512 devices in a mesh: lon: 64 (over x, z_lo, y), lat: 8 (over z_hi, core).
Axes of the slice: x: 4, y: 8, z: 8 (z_hi: 4, z_lo: 2; z = z_hi * 2 + z_lo), core: 2. Of those that a mesh axis runs over, the one named last changes fastest.
Arguments:
- tokens: bfloat16 [1536, 48, 4, 512], P('lon', 'lat'), may hold values from -48 to 48
- cotangent: bfloat16 [1536, 48, 4, 512], P('lon', 'lat'), may hold values from -6 to 6
- w_qkv: bfloat16 [512, 1536], replicated, may hold values from -0.25 to 0.25
- w_out: bfloat16 [512, 512], replicated, may hold values from -0.25 to 0.25
Outputs:
- grad_tokens: bfloat16 [1536, 48, 4, 512], P('lon', 'lat')
- grad_qkv: float32 [786432], P(('lon', 'lat'))
- grad_out: float32 [262144], P(('lon', 'lat'))
The draws below stay inside these ranges and needn't reach their ends.
All inputs are finite; a program needn't handle non-finite values.
Results may differ from the reference program's by a relative error of at most 0.022.
The reference program's roundings to bfloat16 on the way count: a program that leaves them out, or rounds other values in their place, can miss the bound.
Values may be sent and summed in bfloat16 or wider, within the bound.
A program may use at most 64 MiB of HBM per device.

```python
import math
import jax
import jax.numpy as jnp
from jax import lax

D = 512
H = 16
E = 32
WLON = 12
WLAT = 6
WLEV = 2
LEV = 4
NLON = 1536
NLAT = 48
TOKENS = 294912


def draw_tokens(key, part):
    key = jax.random.fold_in(key, 11)
    grid_shape = (NLON, NLAT, LEV, D)
    return jax.random.truncated_normal(key, -6.0, 6.0, grid_shape, jnp.float32).astype(jnp.bfloat16)


def level_of(key, extent, cuts, low, top_value):
    loudness = 1.0
    for position, shards_of in cuts:
        draws = jax.random.uniform(jax.random.fold_in(jax.random.fold_in(key, 6), position), (shards_of,), jnp.float32, low / len(cuts), top_value / len(cuts))
        loudness = loudness * jnp.repeat(jnp.exp(draws), extent[position] // shards_of).reshape((-1,) + (1,) * (len(extent) - 1 - position))
    return loudness


def gaussian(own_key, shape, scale, bound, cuts=(), held_as=jnp.bfloat16):
    array = scale * jax.random.normal(own_key, shape, jnp.float32)
    if cuts:
        array = array * level_of(own_key, shape, cuts, -0.22, 0.18)
    return jnp.clip(array, -bound, bound).astype(held_as)


def setup_inputs(seed: int = 0) -> dict:
    seeds = jax.random.split(jax.random.key(seed), 5)
    tokens = draw_tokens(jax.random.fold_in(seeds[4], 71), 0)
    cotangent = gaussian(seeds[1], (NLON, NLAT, LEV, D), 1.0, 6.0, ((0, 64), (1, 8)))
    w_qkv = gaussian(seeds[2], (D, 3 * H * E), D ** -0.5, 0.25)
    w_out = gaussian(seeds[3], (H * E, D), (H * E) ** -0.5, 0.25)
    return {"tokens": tokens, "cotangent": cotangent, "w_qkv": w_qkv, "w_out": w_out}


def to_windows(grid):
    span_lon, span_lat, span_lev = (grid.shape[0], grid.shape[1], grid.shape[2])
    trailing = grid.shape[3:]
    blocks = grid.reshape((span_lon // WLON, WLON, span_lat // WLAT, WLAT, span_lev // WLEV, WLEV) + trailing)
    axes_order = (0, 2, 4, 1, 3, 5) + tuple(range(6, 6 + len(trailing)))
    return blocks.transpose(axes_order).reshape((-1, WLON * WLAT * WLEV) + trailing)

def from_windows(windows, span_lon, span_lat, span_lev):
    width = windows.shape[-1]
    blocks = windows.reshape(span_lon // WLON, span_lat // WLAT, span_lev // WLEV, WLON, WLAT, WLEV, width)
    return blocks.transpose(0, 3, 1, 4, 2, 5, 6).reshape(span_lon, span_lat, span_lev, width)

def region_grid(lat_shifted, lat_total, levels):
    half_lat = WLAT // 2
    half_lev = WLEV // 2
    lat_orig = (lat_shifted + half_lat) % lat_total
    lat_region = jnp.where(lat_orig < half_lat, 2, jnp.where(lat_orig >= lat_total - (WLAT - half_lat), 1, 0))
    lev_orig = (jnp.arange(levels, dtype=jnp.int32) + half_lev) % levels
    lev_region = jnp.where(lev_orig < half_lev, 2, jnp.where(lev_orig >= levels - (WLEV - half_lev), 1, 0))
    return (lat_region[:, None] * 3 + lev_region[None, :]).astype(jnp.int32)

def window_terms(w_qkv, w_out, carry, inputs):
    win_tokens, win_cotan, win_region = inputs
    seq_len = win_tokens.shape[0]
    inner = H * E
    score_scale = 1.0 / math.sqrt(E)
    projected = jnp.dot(win_tokens, w_qkv, preferred_element_type=jnp.float32).astype(jnp.bfloat16)
    query_part = projected[:, :inner].reshape(seq_len, H, E).astype(jnp.float32)
    key_part = projected[:, inner:2 * inner].reshape(seq_len, H, E).astype(jnp.float32)
    value_part = projected[:, 2 * inner:].reshape(seq_len, H, E).astype(jnp.float32)
    allowed = win_region[:, None] == win_region[None, :]
    scores = jnp.einsum('shd,thd->hst', query_part, key_part) * score_scale
    scores = jnp.where(allowed[None], scores, -1e+30)
    probs = jax.nn.softmax(scores, axis=-1)
    probs_b = probs.astype(jnp.bfloat16)
    attended = jnp.einsum('hst,thd->shd', probs_b.astype(jnp.float32), value_part).astype(jnp.bfloat16).reshape(seq_len, inner)
    mixed = jnp.dot(attended, w_out, preferred_element_type=jnp.float32)
    centred = mixed - lax.optimization_barrier(jnp.mean(mixed, axis=-1, keepdims=True))
    rstd_row = lax.rsqrt(lax.optimization_barrier(jnp.mean(centred * centred, axis=-1, keepdims=True)) + 1e-05)
    normed = centred * rstd_row
    upstream = win_cotan.astype(jnp.float32)
    d_mixed = rstd_row * (upstream - lax.optimization_barrier(jnp.mean(upstream, axis=-1, keepdims=True)) - normed * lax.optimization_barrier(jnp.mean(upstream * normed, axis=-1, keepdims=True)))
    d_mixed = d_mixed.astype(jnp.bfloat16)
    out_term = jnp.dot(attended.T, d_mixed, preferred_element_type=jnp.float32)
    d_attended = jnp.dot(d_mixed, w_out.T, preferred_element_type=jnp.float32).astype(jnp.bfloat16).reshape(seq_len, H, E).astype(jnp.float32)
    d_probs = jnp.einsum('shd,thd->hst', d_attended, value_part)
    d_values = jnp.einsum('hst,shd->thd', probs_b.astype(jnp.float32), d_attended).astype(jnp.bfloat16)
    d_scores = (probs * (d_probs - lax.optimization_barrier(jnp.sum(d_probs * probs, axis=-1, keepdims=True))) * score_scale).astype(jnp.bfloat16).astype(jnp.float32)
    d_query = jnp.einsum('hst,thd->shd', d_scores, key_part).astype(jnp.bfloat16)
    d_keys = jnp.einsum('hst,shd->thd', d_scores, query_part).astype(jnp.bfloat16)
    d_projected = jnp.concatenate([d_query.reshape(seq_len, inner), d_keys.reshape(seq_len, inner), d_values.reshape(seq_len, inner)], axis=-1)
    qkv_term = jnp.dot(win_tokens.T, d_projected, preferred_element_type=jnp.float32)
    path_grad = jnp.dot(d_projected, w_qkv.T, preferred_element_type=jnp.float32).astype(jnp.bfloat16)
    return ((carry[0] + qkv_term, carry[1] + out_term), path_grad)

def reference(tokens, cotangent, w_qkv, w_out):
    shifts = (-(WLON // 2), -(WLAT // 2), -(WLEV // 2))
    shifted_tokens = jnp.roll(tokens, shifts, axis=(0, 1, 2))
    shifted_cotan = jnp.roll(cotangent, shifts, axis=(0, 1, 2))
    regions = region_grid(jnp.arange(NLAT, dtype=jnp.int32), NLAT, LEV)
    regions = jnp.broadcast_to(regions[None], (NLON, NLAT, LEV))
    window_tok = to_windows(shifted_tokens)
    window_cot = to_windows(shifted_cotan)
    window_reg = to_windows(regions)
    initial = (jnp.zeros((D, 3 * H * E), jnp.float32), jnp.zeros((H * E, D), jnp.float32))

    def step_fn(carry, inputs):
        return window_terms(w_qkv, w_out, carry, inputs)
    sums, path_windows = lax.scan(step_fn, initial, (window_tok, window_cot, window_reg))
    path_grid = from_windows(path_windows, NLON, NLAT, LEV)
    path_grid = jnp.roll(path_grid, (WLON // 2, WLAT // 2, WLEV // 2), axis=(0, 1, 2))
    grad_tokens = (cotangent.astype(jnp.float32) + path_grid.astype(jnp.float32)).astype(jnp.bfloat16)
    norm_factor = 1.0 / math.sqrt(TOKENS)
    grad_qkv = (sums[0] * norm_factor).reshape(-1)
    grad_out = (sums[1] * norm_factor).reshape(-1)
    return (grad_tokens, grad_qkv, grad_out)
```

```python
import functools
import math

import jax
import jax.numpy as jnp
from jax import lax
from jax.experimental import pallas as pl
from jax.experimental.pallas import tpu as pltpu
from jax.sharding import PartitionSpec as P

D = 512
H = 16
E = 32
WIN = 144
SLAB = 2 * WIN
TOK = 2 * SLAB
GROUP = 8
LANES = GROUP * WIN
SCALE = 1.0 / math.sqrt(E)
BF = jnp.bfloat16
F32 = jnp.float32
MESH = pl.DeviceIdType.MESH
NN = (((1,), (0,)), ((), ()))
NT = (((1,), (1,)), ((), ()))
TN = (((0,), (0,)), ((), ()))


def mm(a, b, dims=NN):
    return lax.dot_general(a, b, dims, preferred_element_type=F32)


def near(lon, lat):
    n_lon, n_lat = lax.axis_size("lon"), lax.axis_size("lat")
    return ((lax.axis_index("lon") + lon + n_lon) % n_lon, (lax.axis_index("lat") + lat + n_lat) % n_lat)


HALO = ((0, 1), (0, -1), (1, 0), (-1, 0), (1, -1), (-1, 1))


def halo_kernel(tok, cot, ext_tok, ext_cot, send, recv, local):
    barrier = pltpu.get_barrier_semaphore()
    for step in HALO:
        pl.semaphore_signal(barrier, inc=1, device_id=near(*step), device_id_type=MESH)
    pl.semaphore_wait(barrier, len(HALO))
    copies = []
    for a, (src, ext) in enumerate(((tok, ext_tok), (cot, ext_cot))):
        sends = (
            (src.at[6:18, 0:3], ext.at[0, :, 3:6], (0, -1)),
            (src.at[18:24, 3:6], ext.at[1, 0:6, 0:3], (0, 1)),
            (src.at[0:6, 3:6], ext.at[1, 6:12, 0:3], (-1, 1)),
            (src.at[0:6, 0:3], ext.at[1, 6:12, 3:6], (-1, 0)),
        )
        for k, (here, there, step) in enumerate(sends):
            copies.append(
                pltpu.make_async_remote_copy(
                    src_ref=here,
                    dst_ref=there,
                    send_sem=send.at[a, k],
                    recv_sem=recv.at[a, k],
                    device_id=near(*step),
                    device_id_type=MESH,
                )
            )
        copies.append(pltpu.make_async_copy(src.at[6:18, 3:6], ext.at[0, :, 0:3], local.at[a, 0]))
        copies.append(pltpu.make_async_copy(src.at[18:24, 0:3], ext.at[1, 0:6, 3:6], local.at[a, 1]))
    for copy in copies:
        copy.start()
    for copy in copies:
        copy.wait()


def halo(tok, cot):
    any_ = pl.BlockSpec(memory_space=pl.ANY)
    ext = jax.ShapeDtypeStruct((2, 12, 6, 4, D), BF)
    return pl.pallas_call(
        halo_kernel,
        out_shape=(ext, ext),
        in_specs=[any_] * 2,
        out_specs=(any_,) * 2,
        scratch_shapes=[
            pltpu.SemaphoreType.DMA((2, 4)),
            pltpu.SemaphoreType.DMA((2, 4)),
            pltpu.SemaphoreType.DMA((2, 2)),
        ],
        compiler_params=pltpu.CompilerParams(collective_id=0, has_side_effects=True),
        name="halo",
    )(tok, cot)


def lane_head():
    return lax.broadcasted_iota(jnp.int32, (WIN, 256), 1) // E


def stack_heads(x):
    lane = lane_head()
    zero = jnp.zeros_like(x)
    return jnp.concatenate([jnp.where(lane == h, x, zero) for h in range(GROUP)], axis=0)


def pick_heads(r):
    lane = lane_head()
    out = r[0:WIN]
    for h in range(1, GROUP):
        out = jnp.where(lane == h, r[h * WIN : (h + 1) * WIN], out)
    return out


def level_order(rows, natural):
    return natural == 4 * (rows % 72) + (rows // 72 + 1) % 4


def owner_order(i, p):
    x = 2 * ((p // 16) % 2) + (p // 128) % 2
    y = 2 * ((p // 4) % 4) + (p // 64) % 2
    return i == x * 128 + ((p // 32) % 2) * 64 + y * 8 + (p % 4) * 2 + p // 256


def one_hot(relation, shape, swap=False):
    a = lax.broadcasted_iota(jnp.int32, shape, 1 if swap else 0)
    b = lax.broadcasted_iota(jnp.int32, shape, 0 if swap else 1)
    return jnp.where(relation(a, b), 1.0, 0.0).astype(BF)


def region(pos, split_level, split_lat):
    return (pos // 72) * split_level + 2 * split_lat * ((pos % 6) // 3)


def window_kernel(tok, cot, wqkv, wout, path, grad, X, C, PR, A, DM, DA, DP, PT):
    lat = lax.axis_index("lat")
    last = lax.axis_size("lat") - 1
    order = one_hot(level_order, (SLAB, SLAB))
    for w in range(2):
        rows = pl.ds(w * SLAB, SLAB)
        X[rows, :] = mm(order, tok[w].reshape(SLAB, D)).astype(BF)
        C[rows, :] = mm(order, cot[w].reshape(SLAB, D)).astype(BF)
    for c in range(3):
        cols = pl.ds(c * D, D)
        PR[:, cols] = mm(X[...], wqkv[:, cols]).astype(BF)

    def parts(rows, g):
        return [PR[rows, c * D + g * 256 : c * D + (g + 1) * 256] for c in range(3)]

    def forward(i, _):
        rows = pl.ds(pl.multiple_of(i * WIN, WIN), WIN)
        split_lat = jnp.where(lat == jnp.where(i < 2, last, 0), 1, 0)
        key_region = region(lax.broadcasted_iota(jnp.int32, (WIN, 128), 0), i % 2, split_lat)
        for g in range(2):
            q, k, v = parts(rows, g)
            scores = mm(k, stack_heads(q), NT)
            probs_b = []
            for c in range(LANES // 128):
                cols = slice(c * 128, (c + 1) * 128)
                pos = lax.broadcasted_iota(jnp.int32, (1, 128), 1) + c * 128
                allowed = key_region == region(pos % WIN, i % 2, split_lat)
                s = jnp.where(allowed, scores[:, cols] * SCALE, -1e30)
                e = jnp.exp(s - jnp.max(s, axis=0, keepdims=True))
                p = e * (1.0 / jnp.sum(e, axis=0, keepdims=True))
                PT[i * 2 + g, :, cols] = p
                probs_b.append(p.astype(BF))
            probs_b = jnp.concatenate(probs_b, axis=1)
            A[rows, g * 256 : (g + 1) * 256] = pick_heads(mm(probs_b, v, TN)).astype(BF)
        return 0

    lax.fori_loop(0, 4, forward, 0)

    for i in range(4):
        rows = pl.ds(i * WIN, WIN)
        mixed = mm(A[rows, :], wout[...])
        centred = mixed - jnp.mean(mixed, axis=-1, keepdims=True)
        rstd = lax.rsqrt(jnp.mean(centred * centred, axis=-1, keepdims=True) + 1e-5)
        normed = centred * rstd
        up = C[rows, :].astype(F32)
        d_mixed = rstd * (
            up - jnp.mean(up, axis=-1, keepdims=True) - normed * jnp.mean(up * normed, axis=-1, keepdims=True)
        )
        d_mixed = d_mixed.astype(BF)
        DM[rows, :] = d_mixed
        DA[rows, :] = mm(d_mixed, wout[...], NT).astype(BF)

    owner = one_hot(owner_order, (D, D))
    grad[:, :, 3 * D :] = mm(mm(A[...], owner).astype(BF), DM[...], TN).reshape(16, 32, D)

    def backward(i, _):
        rows = pl.ds(pl.multiple_of(i * WIN, WIN), WIN)
        for g in range(2):
            q, k, v = parts(rows, g)
            d_att = stack_heads(DA[rows, g * 256 : (g + 1) * 256])
            d_probs = mm(v, d_att, NT)
            probs_b, d_scores = [], []
            for c in range(LANES // 128):
                cols = slice(c * 128, (c + 1) * 128)
                p = PT[i * 2 + g, :, cols]
                dp = d_probs[:, cols]
                probs_b.append(p.astype(BF))
                d_scores.append((p * (dp - jnp.sum(dp * p, axis=0, keepdims=True)) * SCALE).astype(BF))
            probs_b = jnp.concatenate(probs_b, axis=1)
            d_scores = jnp.concatenate(d_scores, axis=1)
            d_parts = (pick_heads(mm(d_scores, k, TN)), mm(d_scores, stack_heads(q)), mm(probs_b, d_att))
            for c, part in enumerate(d_parts):
                DP[rows, c * D + g * 256 : c * D + (g + 1) * 256] = part.astype(BF)
        return 0

    lax.fori_loop(0, 4, backward, 0)

    X[...] = mm(X[...], owner).astype(BF)
    for c in range(3):
        cols = pl.ds(c * D, D)
        grad[:, :, cols] = mm(X[...], DP[:, cols], TN).reshape(16, 32, D)
    back = one_hot(level_order, (SLAB, SLAB), swap=True)
    for w in range(2):
        grads = mm(DP[pl.ds(w * SLAB, SLAB), :], wqkv[...], NT).astype(BF)
        path[w] = mm(back, grads).astype(BF).reshape(path.shape[1:])


def windows(ext_tok, ext_cot, wqkv, wout):
    vm = pl.BlockSpec(memory_space=pltpu.VMEM)
    rows = pltpu.VMEM((TOK, D), BF)
    wide = pltpu.VMEM((TOK, 3 * D), BF)
    return pl.pallas_call(
        window_kernel,
        out_shape=(jax.ShapeDtypeStruct(ext_tok.shape, BF), jax.ShapeDtypeStruct((16, 32, 4 * D), F32)),
        in_specs=[vm] * 4,
        out_specs=(vm,) * 2,
        scratch_shapes=[rows, rows, wide, rows, rows, rows, wide, pltpu.VMEM((8, WIN, LANES), F32)],
        compiler_params=pltpu.CompilerParams(vmem_limit_bytes=56 * 2**20),
        name="windows",
    )(ext_tok, ext_cot, wqkv, wout)


ROUTES = (
    ("y", "z", "x", 1, 0, 3),
    ("z", "x", "y", 1, 3, 6),
    ("x", "y", "z", 1, 6, 8),
    ("y", "z", "x", -1, 8, 11),
    ("z", "x", "y", -1, 11, 14),
    ("x", "y", "z", -1, 14, 16),
)
SIZES = {"x": 4, "y": 8, "z": 8}
FAR = tuple((a, b, c) for a in (1, 0) for b in (2, 1, 3, 0) for c in (2, 1, 3, 0) if a + b + c)


def position():
    lon, lat = lax.axis_index("lon"), lax.axis_index("lat")
    return {"x": lon // 16, "y": lon % 8, "z": (lat // 2) * 2 + (lon // 8) % 2, "core": lat % 2}


def device(at):
    return (at["x"] * 16 + (at["z"] % 2) * 8 + at["y"], (at["z"] // 2) * 2 + at["core"])


def moved(at, **steps):
    new = dict(at)
    for axis, step in steps.items():
        size = SIZES.get(axis, 2)
        new[axis] = (at[axis] + step + size) % size
    return device(new)


def sum_kernel(path, grad, own_path, total, R0, T, R1, R2, R3, F, Q, s0, r0, s, r, sf, rf, sh, rh, lh):
    at = position()
    bit = {axis: at[axis] % 2 for axis in SIZES}
    core = at["core"]
    others = [near(*step) for step in HALO]
    others += [moved(at, core=1)]
    others += [moved(at, **{axis: step}) for axis in SIZES for step in (1, -1)]
    others += [moved(at, x=2 * a, y=2 * b, z=2 * c) for a, b, c in FAR]
    barrier = pltpu.get_barrier_semaphore()
    for other in others:
        pl.semaphore_signal(barrier, inc=1, device_id=other, device_id_type=MESH)
    pl.semaphore_wait(barrier, len(others))

    def remote(src, dst, send, recv, to):
        copy = pltpu.make_async_remote_copy(
            src_ref=src, dst_ref=dst, send_sem=send, recv_sem=recv, device_id=to, device_id_type=MESH
        )
        copy.start()
        return copy

    first = []
    for n, (_, _, _, _, lo, hi) in enumerate(ROUTES):
        cols = pl.ds(lo * 128, (hi - lo) * 128)
        first.append(
            remote(grad.at[1 - core, :, :, :, :, cols], R0.at[:, :, :, :, cols], s0.at[n], r0.at[n], moved(at, core=1))
        )

    backs = [
        remote(path.at[0, :, 3:6], own_path.at[6:18, 0:3], sh.at[0], rh.at[0], near(0, 1)),
        remote(path.at[1, 0:6, 0:3], own_path.at[18:24, 3:6], sh.at[1], rh.at[1], near(0, -1)),
        remote(path.at[1, 6:12, 0:3], own_path.at[0:6, 3:6], sh.at[2], rh.at[2], near(1, -1)),
        remote(path.at[1, 6:12, 3:6], own_path.at[0:6, 0:3], sh.at[3], rh.at[3], near(1, 0)),
    ]
    locals_ = [
        pltpu.make_async_copy(path.at[0, :, 0:3], own_path.at[6:18, 3:6], lh.at[0]),
        pltpu.make_async_copy(path.at[1, 0:6, 3:6], own_path.at[18:24, 0:3], lh.at[1]),
    ]
    for copy in locals_:
        copy.start()

    def pick(fixed, cols):
        dims = [pl.ds(fixed[axis], 1) if axis in fixed else slice(None) for axis in ("x", "y", "z")]
        return (*dims, slice(None), cols)

    sent = []
    done = [{} for _ in ROUTES]
    flying = list(first)
    for stage in range(4):
        into = (R0, R1, R2, R3)[stage]
        for n, route in enumerate(ROUTES):
            sense, lo, hi = route[3:]
            cols = pl.ds(lo * 128, (hi - lo) * 128)
            flying[n].wait_recv()
            sent.append(flying[n])
            held = pick(done[n], cols)
            if stage == 0:
                T[held] = grad[core, :, :, :, :, cols] + R0[held]
            elif stage < 3:
                T[held] = T[held] + into[held]
            else:
                for c in range(lo, hi):
                    held = pick(done[n], pl.ds(c * 128, 128))
                    F[pl.ds(c, 32, stride=16), :] = (T[held] + into[held]).reshape(32, 128)
            if stage < 3:
                axis = route[stage]
                go = pick({**done[n], axis: 1 - bit[axis]}, cols)
                done[n][axis] = bit[axis]
                flying[n] = remote(
                    T.at[go],
                    (R1, R2, R3)[stage].at[go],
                    s.at[stage, n],
                    r.at[stage, n],
                    moved(at, **{axis: sense * (1 - 2 * bit[axis])}),
                )

    def row(a, b, c):
        place = ((at["x"] // 2 + a) % 2) * 16 + ((at["y"] // 2 + b) % 4) * 4 + (at["z"] // 2 + c) % 4
        return pl.ds(pl.multiple_of(place * 16, 16), 16)

    last = []
    for n, (a, b, c) in enumerate(FAR):
        last.append(
            remote(F.at[row(a, b, c)], Q.at[n], sf.at[n], rf.at[n], moved(at, x=2 * a, y=2 * b, z=2 * c))
        )
    value = F[row(0, 0, 0), :]
    for n, copy in enumerate(last):
        copy.wait_recv()
        value = value + Q[n]
    total[...] = value
    for copy in sent + last:
        copy.wait_send()
    for copy in backs + locals_:
        copy.wait()


def sums(path, grad):
    vm = pl.BlockSpec(memory_space=pltpu.VMEM)
    half = pltpu.VMEM((2, 2, 2, 32, 4 * D), F32)
    dma = pltpu.SemaphoreType.DMA
    n = len(ROUTES)
    return pl.pallas_call(
        sum_kernel,
        out_shape=(jax.ShapeDtypeStruct((24, 6, 4, D), BF), jax.ShapeDtypeStruct((16, 128), F32)),
        in_specs=[vm] * 2,
        out_specs=(vm,) * 2,
        scratch_shapes=[
            *(half,) * 5,
            pltpu.VMEM((32 * 16, 128), F32),
            pltpu.VMEM((len(FAR), 16, 128), F32),
            dma((n,)),
            dma((n,)),
            dma((3, n)),
            dma((3, n)),
            dma((len(FAR),)),
            dma((len(FAR),)),
            dma((4,)),
            dma((4,)),
            dma((2,)),
        ],
        compiler_params=pltpu.CompilerParams(
            collective_id=1, has_side_effects=True, vmem_limit_bytes=56 * 2**20
        ),
        name="sums",
    )(path, grad.reshape(2, 2, 2, 2, 32, 4 * D))


def body(tokens, cotangent, w_qkv, w_out):
    ext_tok, ext_cot = halo(tokens, cotangent)
    path, grad = windows(ext_tok, ext_cot, w_qkv, w_out)
    own_path, total = sums(path, grad)
    grad_tokens = (cotangent.astype(F32) + own_path.astype(F32)).astype(BF)
    count = tokens.shape[0] * tokens.shape[1] * tokens.shape[2] * lax.axis_size("lon") * lax.axis_size("lat")
    total = total.reshape(-1) * (1.0 / math.sqrt(count))
    return grad_tokens, total[: 3 * D], total[3 * D :]


def solution(mesh):
    in_specs = (P("lon", "lat", None, None), P("lon", "lat", None, None), P(), P())
    out_specs = (P("lon", "lat", None, None), P(("lon", "lat")), P(("lon", "lat")))
    return jax.shard_map(body, mesh=mesh, in_specs=in_specs, out_specs=out_specs, check_vma=False)
```

```python
import functools
import math

import jax
import jax.numpy as jnp
from jax import lax
from jax.experimental import pallas as pl
from jax.experimental.pallas import tpu as pltpu
from jax.sharding import PartitionSpec as P

D = 512
H = 16
E = 32
WIN = 144
SLAB = 2 * WIN
TOK = 2 * SLAB
GROUP = 8
LANES = GROUP * WIN
SCALE = 1.0 / math.sqrt(E)
BF = jnp.bfloat16
F32 = jnp.float32
MESH = pl.DeviceIdType.MESH
NN = (((1,), (0,)), ((), ()))
NT = (((1,), (1,)), ((), ()))
TN = (((0,), (0,)), ((), ()))


def mm(a, b, dims=NN):
    return lax.dot_general(a, b, dims, preferred_element_type=F32)


def near(lon, lat):
    n_lon, n_lat = lax.axis_size("lon"), lax.axis_size("lat")
    return ((lax.axis_index("lon") + lon + n_lon) % n_lon, (lax.axis_index("lat") + lat + n_lat) % n_lat)


HALO = ((0, 1), (0, -1), (1, 0), (-1, 0), (1, -1), (-1, 1))
SIZES = {"x": 4, "y": 8, "z": 8}
CUBE = tuple((a, b, c) for a in (1, 0) for b in (1, 0) for c in (1, 0) if a + b + c)
FAR = tuple((a, b, c) for a in (1, 0) for b in (2, 1, 3, 0) for c in (2, 1, 3, 0) if a + b + c)
RELAY = (("y", (2, -2)), ("z", (2, -2)), ("z", (2, -2)), ("x", (2,)))
PARTS = (((0, 2), (2, 4)), ((4, 7), (7, 10)), ((10, 13), (13, 16)))
QKV_BLOCKS = (4, 5, 10, 11, 6, 7, 12, 13, 8, 9, 14, 15)


def position():
    lon, lat = lax.axis_index("lon"), lax.axis_index("lat")
    return {"x": lon // 16, "y": lon % 8, "z": (lat // 2) * 2 + (lon // 8) % 2, "core": lat % 2}


def device(at):
    return (at["x"] * 16 + (at["z"] % 2) * 8 + at["y"], (at["z"] // 2) * 2 + at["core"])


def moved(at, **steps):
    new = dict(at)
    for axis, step in steps.items():
        size = SIZES.get(axis, 2)
        new[axis] = (at[axis] + step + size) % size
    return device(new)


def lane_head():
    return lax.broadcasted_iota(jnp.int32, (WIN, 256), 1) // E


def stack_heads(x):
    lane = lane_head()
    zero = jnp.zeros_like(x)
    return jnp.concatenate([jnp.where(lane == h, x, zero) for h in range(GROUP)], axis=0)


def pick_heads(r):
    lane = lane_head()
    out = r[0:WIN]
    for h in range(1, GROUP):
        out = jnp.where(lane == h, r[h * WIN : (h + 1) * WIN], out)
    return out


def level_order(rows, natural):
    return natural == 4 * (rows % 72) + (rows // 72 + 1) % 4


def owner_order(i, p):
    x = 2 * ((p // 16) % 2) + (p // 128) % 2
    y = 2 * ((p // 4) % 4) + (p // 64) % 2
    return i == x * 128 + ((p // 32) % 2) * 64 + y * 8 + (p % 4) * 2 + p // 256


def one_hot(relation, shape, swap=False):
    a = lax.broadcasted_iota(jnp.int32, shape, 1 if swap else 0)
    b = lax.broadcasted_iota(jnp.int32, shape, 0 if swap else 1)
    return jnp.where(relation(a, b), 1.0, 0.0).astype(BF)


def region(pos, split_level, split_lat):
    return (pos // 72) * split_level + 2 * split_lat * ((pos % 6) // 3)


def signal(sem, to):
    pl.semaphore_signal(sem, inc=1, device_id=to, device_id_type=MESH)


def remote(src, dst, send, recv, to):
    copy = pltpu.make_async_remote_copy(
        src_ref=src, dst_ref=dst, send_sem=send, recv_sem=recv, device_id=to, device_id_type=MESH
    )
    copy.start()
    return copy


def local(src, dst, sem):
    copy = pltpu.make_async_copy(src, dst, sem)
    copy.start()
    return copy


def block_kernel(norm, tok, cot, wqkv, wout, own_path, grad_qkv, grad_out, *scratch):
    (ET, EC, X, XO, C, PR, A, DM, DA, DP, PT, path, G, R0, RC, F, Q) = scratch[:17]
    (hs, hr, hl, bs, br, bl, s0, r0, sc, rc, sf, rf, relay) = scratch[17:]
    at = position()
    bit = {axis: at[axis] % 2 for axis in SIZES}
    core = at["core"]
    lat = lax.axis_index("lat")
    last = lax.axis_size("lat") - 1

    greeted = [near(*step) for step in HALO] + [moved(at, core=1)]
    for a, b, c in CUBE:
        for sense in (1, -1):
            steps = {axis: sense * far * (1 - 2 * bit[axis]) for axis, far in (("x", a), ("y", b), ("z", c))}
            greeted.append(moved(at, **steps))
    greeted += [moved(at, **{axis: step}) for axis, steps in RELAY[1:] + RELAY[:1] for step in steps][2:]
    barrier = pltpu.get_barrier_semaphore()
    for other in greeted:
        signal(barrier, other)
    pl.semaphore_wait(barrier, len(greeted))

    come = []
    for a, (src, ext) in enumerate(((tok, ET), (cot, EC))):
        come.append(
            (
                local(src.at[6:18, 3:6], ext.at[0, :, 0:3], hl.at[a, 0]),
                remote(src.at[6:18, 0:3], ext.at[0, :, 3:6], hs.at[a, 0], hr.at[a, 0], near(0, -1)),
            )
        )
        come.append(
            (
                local(src.at[18:24, 0:3], ext.at[1, 0:6, 3:6], hl.at[a, 1]),
                remote(src.at[18:24, 3:6], ext.at[1, 0:6, 0:3], hs.at[a, 1], hr.at[a, 1], near(0, 1)),
                remote(src.at[0:6, 3:6], ext.at[1, 6:12, 0:3], hs.at[a, 2], hr.at[a, 2], near(-1, 1)),
                remote(src.at[0:6, 0:3], ext.at[1, 6:12, 3:6], hs.at[a, 3], hr.at[a, 3], near(-1, 0)),
            )
        )

    def relay_send(n):
        axis, steps = RELAY[n]
        for step in steps:
            signal(relay.at[n], moved(at, **{axis: step}))

    def relay_wait(n):
        pl.semaphore_wait(relay.at[n], len(RELAY[n][1]))

    relay_send(0)
    order = one_hot(level_order, (SLAB, SLAB))
    owner = one_hot(owner_order, (D, D), swap=True)

    def parts(rows, g):
        return [PR[rows, c * D + g * 256 : c * D + (g + 1) * 256] for c in range(3)]

    def forward(i, _):
        rows = pl.ds(pl.multiple_of(i * WIN, WIN), WIN)
        split_lat = jnp.where(lat == jnp.where(i < 2, last, 0), 1, 0)
        key_region = region(lax.broadcasted_iota(jnp.int32, (WIN, 128), 0), i % 2, split_lat)
        for g in range(2):
            q, k, v = parts(rows, g)
            scores = mm(k, stack_heads(q), NT)
            probs_b = []
            for c in range(LANES // 128):
                cols = slice(c * 128, (c + 1) * 128)
                pos = lax.broadcasted_iota(jnp.int32, (1, 128), 1) + c * 128
                allowed = key_region == region(pos % WIN, i % 2, split_lat)
                s = jnp.where(allowed, scores[:, cols] * SCALE, -1e30)
                e = jnp.exp(s - jnp.max(s, axis=0, keepdims=True))
                p = e * (1.0 / jnp.sum(e, axis=0, keepdims=True))
                PT[i * 2 + g, :, cols] = p
                probs_b.append(p.astype(BF))
            probs_b = jnp.concatenate(probs_b, axis=1)
            A[rows, g * 256 : (g + 1) * 256] = pick_heads(mm(probs_b, v, TN)).astype(BF)
        return 0

    for w in range(2):
        for copy in come[w]:
            copy.wait()
        rows = pl.ds(w * SLAB, SLAB)
        X[rows, :] = mm(order, ET[w].reshape(SLAB, D)).astype(BF)
        for c in range(3):
            cols = pl.ds(c * D, D)
            PR[rows, cols] = mm(X[rows, :], wqkv[:, cols]).astype(BF)
        lax.fori_loop(2 * w, 2 * w + 2, forward, 0)
        relay_wait(w)
        relay_send(w + 1)

    XO[...] = mm(owner, X[...], NT).astype(BF)
    for w in range(2):
        for copy in come[2 + w]:
            copy.wait()
        rows = pl.ds(w * SLAB, SLAB)
        C[rows, :] = mm(order, EC[w].reshape(SLAB, D)).astype(BF)
    for i in range(4):
        rows = pl.ds(i * WIN, WIN)
        mixed = mm(A[rows, :], wout[...])
        centred = mixed - jnp.mean(mixed, axis=-1, keepdims=True)
        rstd = lax.rsqrt(jnp.mean(centred * centred, axis=-1, keepdims=True) + 1e-5)
        normed = centred * rstd
        up = C[rows, :].astype(F32)
        d_mixed = rstd * (
            up - jnp.mean(up, axis=-1, keepdims=True) - normed * jnp.mean(up * normed, axis=-1, keepdims=True)
        )
        d_mixed = d_mixed.astype(BF)
        DM[rows, :] = d_mixed
        DA[rows, :] = mm(d_mixed, wout[...], NT).astype(BF)

    sent = []

    def span(lo, hi):
        return pl.ds(lo * 128, (hi - lo) * 128)

    def to_core(part):
        return [
            remote(
                G.at[1 - core, :, :, :, :, span(lo, hi)],
                R0.at[:, :, :, :, span(lo, hi)],
                s0.at[part, n],
                r0.at[part, n],
                moved(at, core=1),
            )
            for n, (lo, hi) in enumerate(PARTS[part])
        ]

    def to_cube(part, flying):
        out = []
        for n, (lo, hi) in enumerate(PARTS[part]):
            flying[n].wait_recv()
            sent.append(flying[n])
            cols = span(lo, hi)
            G[core, :, :, :, :, cols] = G[core, :, :, :, :, cols] + R0[:, :, :, :, cols]
            for k, (a, b, c) in enumerate(CUBE):
                steps = {
                    axis: far * (1 - 2 * n) * (1 - 2 * bit[axis]) for axis, far in (("x", a), ("y", b), ("z", c)) if far
                }
                place = [1 - bit[axis] if far else bit[axis] for axis, far in (("x", a), ("y", b), ("z", c))]
                out.append(
                    remote(
                        G.at[core, place[0], place[1], place[2], :, cols],
                        RC.at[k, :, cols],
                        sc.at[part, n, k],
                        rc.at[part, n, k],
                        moved(at, **steps),
                    )
                )
        return out

    def take_cube(part, flying):
        for copy in flying:
            copy.wait_recv()
        sent.extend(flying)
        for c in range(PARTS[part][0][0], PARTS[part][1][1]):
            cols = span(c, c + 1)
            value = G[core, bit["x"], bit["y"], bit["z"], :, cols]
            for k in range(len(CUBE)):
                value = value + RC[k, :, cols]
            F[c // 8, pl.ds(c % 8, 32, stride=8), :] = value

    def row(a, b, c):
        place = ((at["x"] // 2 + a) % 2) * 16 + ((at["y"] // 2 + b) % 4) * 4 + (at["z"] // 2 + c) % 4
        return pl.ds(pl.multiple_of(place * 8, 8), 8)

    def to_far(half):
        return [
            remote(
                F.at[half, row(a, b, c)],
                Q.at[half, n],
                sf.at[half, n],
                rf.at[half, n],
                moved(at, x=2 * a, y=2 * b, z=2 * c),
            )
            for n, (a, b, c) in enumerate(FAR)
        ]

    def take_far(half, flying):
        value = F[half, row(0, 0, 0), :]
        for n, copy in enumerate(flying):
            copy.wait_recv()
            value = value + Q[half, n]
        sent.extend(flying)
        return value * norm

    def backward(g, i, _):
        rows = pl.ds(pl.multiple_of(i * WIN, WIN), WIN)
        q, k, v = parts(rows, g)
        d_att = stack_heads(DA[rows, g * 256 : (g + 1) * 256])
        d_probs = mm(v, d_att, NT)
        probs_b, d_scores = [], []
        for c in range(LANES // 128):
            cols = slice(c * 128, (c + 1) * 128)
            p = PT[i * 2 + g, :, cols]
            dp = d_probs[:, cols]
            probs_b.append(p.astype(BF))
            d_scores.append((p * (dp - jnp.sum(dp * p, axis=0, keepdims=True)) * SCALE).astype(BF))
        probs_b = jnp.concatenate(probs_b, axis=1)
        d_scores = jnp.concatenate(d_scores, axis=1)
        d_parts = (pick_heads(mm(d_scores, k, TN)), mm(d_scores, stack_heads(q)), mm(probs_b, d_att))
        for c, part in enumerate(d_parts):
            DP[rows, c * D + g * 256 : c * D + (g + 1) * 256] = part.astype(BF)
        return 0

    def weight_grad(g):
        for c in range(3):
            G[:, :, :, :, :, span(4 + 6 * g + 2 * c, 6 + 6 * g + 2 * c)] = mm(
                XO[...], DP[:, c * D + g * 256 : c * D + (g + 1) * 256]
            ).reshape(2, 2, 2, 2, 32, 256)

    G[:, :, :, :, :, 0:D] = mm(mm(owner, A[...], NT).astype(BF), DM[...]).reshape(2, 2, 2, 2, 32, D)
    core_out = to_core(0)
    relay_wait(2)
    relay_send(3)
    lax.fori_loop(0, 2, functools.partial(backward, 0), 0)
    cube_out = to_cube(0, core_out)
    lax.fori_loop(2, 4, functools.partial(backward, 0), 0)
    weight_grad(0)
    core_first = to_core(1)
    relay_wait(3)
    lax.fori_loop(0, 2, functools.partial(backward, 1), 0)
    cube_first = to_cube(1, core_first)
    take_cube(0, cube_out)
    lax.fori_loop(2, 4, functools.partial(backward, 1), 0)
    weight_grad(1)
    core_second = to_core(2)

    back = one_hot(level_order, (SLAB, SLAB), swap=True)
    backs = []
    for w in range(2):
        grads = mm(DP[pl.ds(w * SLAB, SLAB), :], wqkv[...], NT).astype(BF)
        path[w] = mm(back, grads).astype(BF).reshape(path.shape[1:])
        if w == 0:
            backs += [
                remote(path.at[0, :, 3:6], own_path.at[6:18, 0:3], bs.at[0], br.at[0], near(0, 1)),
                local(path.at[0, :, 0:3], own_path.at[6:18, 3:6], bl.at[0]),
            ]
        else:
            backs += [
                remote(path.at[1, 0:6, 0:3], own_path.at[18:24, 3:6], bs.at[1], br.at[1], near(0, -1)),
                remote(path.at[1, 6:12, 0:3], own_path.at[0:6, 3:6], bs.at[2], br.at[2], near(1, -1)),
                remote(path.at[1, 6:12, 3:6], own_path.at[0:6, 0:3], bs.at[3], br.at[3], near(1, 0)),
                local(path.at[1, 0:6, 3:6], own_path.at[18:24, 0:3], bl.at[1]),
            ]

    cube_second = to_cube(2, core_second)
    take_cube(1, cube_first)
    far_first = to_far(0)
    take_cube(2, cube_second)
    far_second = to_far(1)
    low = take_far(0, far_first)
    high = take_far(1, far_second)
    grad_out[...] = low[0:4]
    for n, block in enumerate(QKV_BLOCKS):
        grad_qkv[n : n + 1, :] = (low, high)[block // 8][block % 8 : block % 8 + 1]
    for copy in sent:
        copy.wait_send()
    for copy in backs:
        copy.wait()


def block(tok, cot, wqkv, wout, norm):
    vm = pl.BlockSpec(memory_space=pltpu.VMEM)
    any_ = pl.BlockSpec(memory_space=pl.ANY)
    rows = pltpu.VMEM((TOK, D), BF)
    wide = pltpu.VMEM((TOK, 3 * D), BF)
    ext = pltpu.VMEM((2, 12, 6, 4, D), BF)
    dma = pltpu.SemaphoreType.DMA
    return pl.pallas_call(
        functools.partial(block_kernel, norm),
        out_shape=(
            jax.ShapeDtypeStruct(tok.shape, BF),
            jax.ShapeDtypeStruct((12, 128), F32),
            jax.ShapeDtypeStruct((4, 128), F32),
        ),
        in_specs=[any_, any_, vm, vm],
        out_specs=(vm,) * 3,
        scratch_shapes=[
            ext,
            ext,
            rows,
            pltpu.VMEM((D, TOK), BF),
            rows,
            wide,
            rows,
            rows,
            rows,
            wide,
            pltpu.VMEM((8, WIN, LANES), F32),
            ext,
            pltpu.VMEM((2, 2, 2, 2, 32, 4 * D), F32),
            pltpu.VMEM((2, 2, 2, 32, 4 * D), F32),
            pltpu.VMEM((len(CUBE), 32, 4 * D), F32),
            pltpu.VMEM((2, 32 * 8, 128), F32),
            pltpu.VMEM((2, len(FAR), 8, 128), F32),
            dma((2, 4)),
            dma((2, 4)),
            dma((2, 2)),
            dma((4,)),
            dma((4,)),
            dma((2,)),
            dma((3, 2)),
            dma((3, 2)),
            dma((3, 2, len(CUBE))),
            dma((3, 2, len(CUBE))),
            dma((2, len(FAR))),
            dma((2, len(FAR))),
            pltpu.SemaphoreType.REGULAR((len(RELAY),)),
        ],
        compiler_params=pltpu.CompilerParams(collective_id=0, has_side_effects=True, vmem_limit_bytes=56 * 2**20),
        name="block",
    )(tok, cot, wqkv, wout)


def body(tokens, cotangent, w_qkv, w_out):
    count = tokens.shape[0] * tokens.shape[1] * tokens.shape[2] * lax.axis_size("lon") * lax.axis_size("lat")
    own_path, grad_qkv, grad_out = block(tokens, cotangent, w_qkv, w_out, 1.0 / math.sqrt(count))
    grad_tokens = (cotangent.astype(F32) + own_path.astype(F32)).astype(BF)
    return grad_tokens, grad_qkv.reshape(-1), grad_out.reshape(-1)


def solution(mesh):
    in_specs = (P("lon", "lat", None, None), P("lon", "lat", None, None), P(), P())
    out_specs = (P("lon", "lat", None, None), P(("lon", "lat")), P(("lon", "lat")))
    return jax.shard_map(body, mesh=mesh, in_specs=in_specs, out_specs=out_specs, check_vma=False)
```

```python
import functools
import math

import jax
import jax.numpy as jnp
from jax import lax
from jax.experimental import pallas as pl
from jax.experimental.pallas import tpu as pltpu
from jax.sharding import PartitionSpec as P

D = 512
H = 16
E = 32
WIN = 144
SLAB = 2 * WIN
TOK = 2 * SLAB
GROUP = 8
LANES = GROUP * WIN
SCALE = 1.0 / math.sqrt(E)
BF = jnp.bfloat16
F32 = jnp.float32
MESH = pl.DeviceIdType.MESH
NN = (((1,), (0,)), ((), ()))
NT = (((1,), (1,)), ((), ()))
TN = (((0,), (0,)), ((), ()))


def mm(a, b, dims=NN):
    return lax.dot_general(a, b, dims, preferred_element_type=F32)


def near(lon, lat):
    n_lon, n_lat = lax.axis_size("lon"), lax.axis_size("lat")
    return ((lax.axis_index("lon") + lon + n_lon) % n_lon, (lax.axis_index("lat") + lat + n_lat) % n_lat)


HALO = ((0, 1), (0, -1), (1, 0), (-1, 0), (1, -1), (-1, 1))
SIZES = {"x": 4, "y": 8, "z": 8}
CUBE = tuple((a, b, c) for a in (1, 0) for b in (1, 0) for c in (1, 0) if a + b + c)
FAR = tuple((a, b, c) for a in (1, 0) for b in (2, 1, 3, 0) for c in (2, 1, 3, 0) if a + b + c)
RELAY = (("y", (2, -2)), ("z", (2, -2)), ("z", (2, -2)), ("x", (2,)))
PARTS = (((0, 2), (2, 4)), ((4, 7), (7, 10)), ((10, 13), (13, 16)))
QKV_BLOCKS = (4, 5, 10, 11, 6, 7, 12, 13, 8, 9, 14, 15)


def position():
    lon, lat = lax.axis_index("lon"), lax.axis_index("lat")
    return {"x": lon // 16, "y": lon % 8, "z": (lat // 2) * 2 + (lon // 8) % 2, "core": lat % 2}


def device(at):
    return (at["x"] * 16 + (at["z"] % 2) * 8 + at["y"], (at["z"] // 2) * 2 + at["core"])


def moved(at, **steps):
    new = dict(at)
    for axis, step in steps.items():
        size = SIZES.get(axis, 2)
        new[axis] = (at[axis] + step + size) % size
    return device(new)


def lane_head():
    return lax.broadcasted_iota(jnp.int32, (WIN, 256), 1) // E


def stack_heads(x):
    lane = lane_head()
    zero = jnp.zeros_like(x)
    return jnp.concatenate([jnp.where(lane == h, x, zero) for h in range(GROUP)], axis=0)


def pick_heads(r):
    lane = lane_head()
    out = r[0:WIN]
    for h in range(1, GROUP):
        out = jnp.where(lane == h, r[h * WIN : (h + 1) * WIN], out)
    return out


def level_order(rows, natural):
    return natural == 4 * (rows % 72) + (rows // 72 + 1) % 4


def owner_order(i, p):
    x = 2 * ((p // 16) % 2) + (p // 128) % 2
    y = 2 * ((p // 4) % 4) + (p // 64) % 2
    return i == x * 128 + ((p // 32) % 2) * 64 + y * 8 + (p % 4) * 2 + p // 256


def one_hot(relation, shape, swap=False):
    a = lax.broadcasted_iota(jnp.int32, shape, 1 if swap else 0)
    b = lax.broadcasted_iota(jnp.int32, shape, 0 if swap else 1)
    return jnp.where(relation(a, b), 1.0, 0.0).astype(BF)


def region(pos, split_level, split_lat):
    return (pos // 72) * split_level + 2 * split_lat * ((pos % 6) // 3)


def signal(sem, to):
    pl.semaphore_signal(sem, inc=1, device_id=to, device_id_type=MESH)


def remote(src, dst, send, recv, to):
    copy = pltpu.make_async_remote_copy(
        src_ref=src, dst_ref=dst, send_sem=send, recv_sem=recv, device_id=to, device_id_type=MESH
    )
    copy.start()
    return copy


def local(src, dst, sem):
    copy = pltpu.make_async_copy(src, dst, sem)
    copy.start()
    return copy


def block_kernel(norm, tok, cot, wqkv_in, wout_in, grad_tok, grad_qkv, grad_out, *scratch):
    (wqkv, wout, CT, own_path, ET, EC, X, XO, C, PR, A, DM, DA, DP, PT, path, G, R0, CB, RC, F, Q) = scratch[:22]
    (ws, hs, hr, hl, bs, br, bl, s0, r0, sc, rc, sf, rf, relay) = scratch[22:]
    at = position()
    bit = {axis: at[axis] % 2 for axis in SIZES}
    core = at["core"]
    lat = lax.axis_index("lat")
    last = lax.axis_size("lat") - 1

    greeted = [near(*step) for step in HALO] + [moved(at, core=1)]
    for a, b, c in CUBE:
        for sense in (1, -1):
            steps = {axis: sense * far * (1 - 2 * bit[axis]) for axis, far in (("x", a), ("y", b), ("z", c))}
            greeted.append(moved(at, **steps))
    greeted += [moved(at, **{axis: step}) for axis, steps in RELAY[1:] + RELAY[:1] for step in steps][2:]
    barrier = pltpu.get_barrier_semaphore()
    for other in greeted:
        signal(barrier, other)
    own = [local(wqkv_in, wqkv, ws.at[0]), local(wout_in, wout, ws.at[1]), local(cot, CT, ws.at[2])]
    pl.semaphore_wait(barrier, len(greeted))

    come = []
    for a, (src, ext) in enumerate(((tok, ET), (cot, EC))):
        come.append(
            (
                local(src.at[6:18, 3:6], ext.at[0, :, 0:3], hl.at[a, 0]),
                remote(src.at[6:18, 0:3], ext.at[0, :, 3:6], hs.at[a, 0], hr.at[a, 0], near(0, -1)),
            )
        )
        come.append(
            (
                local(src.at[18:24, 0:3], ext.at[1, 0:6, 3:6], hl.at[a, 1]),
                remote(src.at[18:24, 3:6], ext.at[1, 0:6, 0:3], hs.at[a, 1], hr.at[a, 1], near(0, 1)),
                remote(src.at[0:6, 3:6], ext.at[1, 6:12, 0:3], hs.at[a, 2], hr.at[a, 2], near(-1, 1)),
                remote(src.at[0:6, 0:3], ext.at[1, 6:12, 3:6], hs.at[a, 3], hr.at[a, 3], near(-1, 0)),
            )
        )

    def relay_send(n):
        axis, steps = RELAY[n]
        for step in steps:
            signal(relay.at[n], moved(at, **{axis: step}))

    def relay_wait(n):
        pl.semaphore_wait(relay.at[n], len(RELAY[n][1]))

    relay_send(0)
    own[0].wait()
    order = one_hot(level_order, (SLAB, SLAB))
    owner = one_hot(owner_order, (D, D), swap=True)

    def parts(rows, g):
        return [PR[rows, c * D + g * 256 : c * D + (g + 1) * 256] for c in range(3)]

    def forward(i, _):
        rows = pl.ds(pl.multiple_of(i * WIN, WIN), WIN)
        split_lat = jnp.where(lat == jnp.where(i < 2, last, 0), 1, 0)
        key_region = region(lax.broadcasted_iota(jnp.int32, (WIN, 128), 0), i % 2, split_lat)
        for g in range(2):
            q, k, v = parts(rows, g)
            scores = mm(k, stack_heads(q), NT)
            probs_b = []
            for c in range(LANES // 128):
                cols = slice(c * 128, (c + 1) * 128)
                pos = lax.broadcasted_iota(jnp.int32, (1, 128), 1) + c * 128
                allowed = key_region == region(pos % WIN, i % 2, split_lat)
                s = jnp.where(allowed, scores[:, cols] * SCALE, -1e30)
                e = jnp.exp(s - jnp.max(s, axis=0, keepdims=True))
                p = e * (1.0 / jnp.sum(e, axis=0, keepdims=True))
                PT[i * 2 + g, :, cols] = p
                probs_b.append(p.astype(BF))
            probs_b = jnp.concatenate(probs_b, axis=1)
            A[rows, g * 256 : (g + 1) * 256] = pick_heads(mm(probs_b, v, TN)).astype(BF)
        return 0

    for w in range(2):
        for copy in come[w]:
            copy.wait()
        rows = pl.ds(w * SLAB, SLAB)
        X[rows, :] = mm(order, ET[w].reshape(SLAB, D)).astype(BF)
        for c in range(3):
            cols = pl.ds(c * D, D)
            PR[rows, cols] = mm(X[rows, :], wqkv[:, cols]).astype(BF)
        lax.fori_loop(2 * w, 2 * w + 2, forward, 0)
        relay_wait(w)
        relay_send(w + 1)

    XO[...] = mm(owner, X[...], NT).astype(BF)
    own[1].wait()
    for w in range(2):
        for copy in come[2 + w]:
            copy.wait()
        rows = pl.ds(w * SLAB, SLAB)
        C[rows, :] = mm(order, EC[w].reshape(SLAB, D)).astype(BF)
    for i in range(4):
        rows = pl.ds(i * WIN, WIN)
        mixed = mm(A[rows, :], wout[...])
        centred = mixed - jnp.mean(mixed, axis=-1, keepdims=True)
        rstd = lax.rsqrt(jnp.mean(centred * centred, axis=-1, keepdims=True) + 1e-5)
        normed = centred * rstd
        up = C[rows, :].astype(F32)
        d_mixed = rstd * (
            up - jnp.mean(up, axis=-1, keepdims=True) - normed * jnp.mean(up * normed, axis=-1, keepdims=True)
        )
        d_mixed = d_mixed.astype(BF)
        DM[rows, :] = d_mixed
        DA[rows, :] = mm(d_mixed, wout[...], NT).astype(BF)

    sent = []

    def span(lo, hi):
        return pl.ds(lo * 128, (hi - lo) * 128)

    def to_core(part):
        return [
            remote(
                G.at[1 - core, :, :, :, :, span(lo, hi)],
                R0.at[:, :, :, :, span(lo, hi)],
                s0.at[part, n],
                r0.at[part, n],
                moved(at, core=1),
            )
            for n, (lo, hi) in enumerate(PARTS[part])
        ]

    def to_cube(part, flying):
        out = []
        for n, (lo, hi) in enumerate(PARTS[part]):
            flying[n].wait_recv()
            sent.append(flying[n])
            cols = span(lo, hi)
            CB[:, :, :, :, cols] = (G[core, :, :, :, :, cols] + R0[:, :, :, :, cols]).astype(BF)
            for k, (a, b, c) in enumerate(CUBE):
                steps = {
                    axis: far * (1 - 2 * n) * (1 - 2 * bit[axis]) for axis, far in (("x", a), ("y", b), ("z", c)) if far
                }
                place = [1 - bit[axis] if far else bit[axis] for axis, far in (("x", a), ("y", b), ("z", c))]
                out.append(
                    remote(
                        CB.at[place[0], place[1], place[2], :, cols],
                        RC.at[k, :, cols],
                        sc.at[part, n, k],
                        rc.at[part, n, k],
                        moved(at, **steps),
                    )
                )
        return out

    def take_cube(part, flying):
        for copy in flying:
            copy.wait_recv()
        sent.extend(flying)
        for c in range(PARTS[part][0][0], PARTS[part][1][1]):
            cols = span(c, c + 1)
            value = G[core, bit["x"], bit["y"], bit["z"], :, cols] + R0[bit["x"], bit["y"], bit["z"], :, cols]
            for k in range(len(CUBE)):
                value = value + RC[k, :, cols].astype(F32)
            F[c // 8, pl.ds(c % 8, 32, stride=8), :] = value

    def row(a, b, c):
        place = ((at["x"] // 2 + a) % 2) * 16 + ((at["y"] // 2 + b) % 4) * 4 + (at["z"] // 2 + c) % 4
        return pl.ds(pl.multiple_of(place * 8, 8), 8)

    def to_far(half):
        return [
            remote(
                F.at[half, row(a, b, c)],
                Q.at[half, n],
                sf.at[half, n],
                rf.at[half, n],
                moved(at, x=2 * a, y=2 * b, z=2 * c),
            )
            for n, (a, b, c) in enumerate(FAR)
        ]

    def take_far(half, flying):
        value = F[half, row(0, 0, 0), :]
        for n, copy in enumerate(flying):
            copy.wait_recv()
            value = value + Q[half, n]
        sent.extend(flying)
        return value * norm

    def backward(g, i, _):
        rows = pl.ds(pl.multiple_of(i * WIN, WIN), WIN)
        q, k, v = parts(rows, g)
        d_att = stack_heads(DA[rows, g * 256 : (g + 1) * 256])
        d_probs = mm(v, d_att, NT)
        probs_b, d_scores = [], []
        for c in range(LANES // 128):
            cols = slice(c * 128, (c + 1) * 128)
            p = PT[i * 2 + g, :, cols]
            dp = d_probs[:, cols]
            probs_b.append(p.astype(BF))
            d_scores.append((p * (dp - jnp.sum(dp * p, axis=0, keepdims=True)) * SCALE).astype(BF))
        probs_b = jnp.concatenate(probs_b, axis=1)
        d_scores = jnp.concatenate(d_scores, axis=1)
        d_parts = (pick_heads(mm(d_scores, k, TN)), mm(d_scores, stack_heads(q)), mm(probs_b, d_att))
        for c, part in enumerate(d_parts):
            DP[rows, c * D + g * 256 : c * D + (g + 1) * 256] = part.astype(BF)
        return 0

    def weight_grad(g):
        for c in range(3):
            G[:, :, :, :, :, span(4 + 6 * g + 2 * c, 6 + 6 * g + 2 * c)] = mm(
                XO[...], DP[:, c * D + g * 256 : c * D + (g + 1) * 256]
            ).reshape(2, 2, 2, 2, 32, 256)

    G[:, :, :, :, :, 0:D] = mm(mm(owner, A[...], NT).astype(BF), DM[...]).reshape(2, 2, 2, 2, 32, D)
    core_out = to_core(0)
    relay_wait(2)
    relay_send(3)
    lax.fori_loop(0, 2, functools.partial(backward, 0), 0)
    cube_out = to_cube(0, core_out)
    lax.fori_loop(2, 4, functools.partial(backward, 0), 0)
    weight_grad(0)
    core_first = to_core(1)
    relay_wait(3)
    lax.fori_loop(0, 2, functools.partial(backward, 1), 0)
    cube_first = to_cube(1, core_first)
    take_cube(0, cube_out)
    lax.fori_loop(2, 4, functools.partial(backward, 1), 0)
    weight_grad(1)
    core_second = to_core(2)

    back = one_hot(level_order, (SLAB, SLAB), swap=True)
    backs = []
    for w in range(2):
        grads = mm(DP[pl.ds(w * SLAB, SLAB), :], wqkv[...], NT).astype(BF)
        path[w] = mm(back, grads).astype(BF).reshape(path.shape[1:])
        if w == 0:
            backs += [
                remote(path.at[0, :, 3:6], own_path.at[6:18, 0:3], bs.at[0], br.at[0], near(0, 1)),
                local(path.at[0, :, 0:3], own_path.at[6:18, 3:6], bl.at[0]),
            ]
        else:
            backs += [
                remote(path.at[1, 0:6, 0:3], own_path.at[18:24, 3:6], bs.at[1], br.at[1], near(0, -1)),
                remote(path.at[1, 6:12, 0:3], own_path.at[0:6, 3:6], bs.at[2], br.at[2], near(1, -1)),
                remote(path.at[1, 6:12, 3:6], own_path.at[0:6, 0:3], bs.at[3], br.at[3], near(1, 0)),
                local(path.at[1, 0:6, 3:6], own_path.at[18:24, 0:3], bl.at[1]),
            ]

    cube_second = to_cube(2, core_second)
    take_cube(1, cube_first)
    far_first = to_far(0)
    take_cube(2, cube_second)
    far_second = to_far(1)
    for copy in backs:
        copy.wait()
    own[2].wait()

    def add(i, _):
        CT[i] = (CT[i].astype(F32) + own_path[i].astype(F32)).astype(BF)
        return 0

    lax.fori_loop(0, CT.shape[0], add, 0)
    out = local(CT, grad_tok, ws.at[3])
    low = take_far(0, far_first)
    high = take_far(1, far_second)
    grad_out[...] = low[0:4]
    for n, block in enumerate(QKV_BLOCKS):
        grad_qkv[n : n + 1, :] = (low, high)[block // 8][block % 8 : block % 8 + 1]
    for copy in sent:
        copy.wait_send()
    out.wait()


def block(tok, cot, wqkv, wout, norm):
    vm = pl.BlockSpec(memory_space=pltpu.VMEM)
    any_ = pl.BlockSpec(memory_space=pl.ANY)
    rows = pltpu.VMEM((TOK, D), BF)
    wide = pltpu.VMEM((TOK, 3 * D), BF)
    ext = pltpu.VMEM((2, 12, 6, 4, D), BF)
    dma = pltpu.SemaphoreType.DMA
    return pl.pallas_call(
        functools.partial(block_kernel, norm),
        out_shape=(
            jax.ShapeDtypeStruct(tok.shape, BF),
            jax.ShapeDtypeStruct((12, 128), F32),
            jax.ShapeDtypeStruct((4, 128), F32),
        ),
        in_specs=[any_] * 4,
        out_specs=(any_, vm, vm),
        scratch_shapes=[
            pltpu.VMEM(wqkv.shape, BF),
            pltpu.VMEM(wout.shape, BF),
            pltpu.VMEM(tok.shape, BF),
            pltpu.VMEM(tok.shape, BF),
            ext,
            ext,
            rows,
            pltpu.VMEM((D, TOK), BF),
            rows,
            wide,
            rows,
            rows,
            rows,
            wide,
            pltpu.VMEM((8, WIN, LANES), F32),
            ext,
            pltpu.VMEM((2, 2, 2, 2, 32, 4 * D), F32),
            pltpu.VMEM((2, 2, 2, 32, 4 * D), F32),
            pltpu.VMEM((2, 2, 2, 32, 4 * D), BF),
            pltpu.VMEM((len(CUBE), 32, 4 * D), BF),
            pltpu.VMEM((2, 32 * 8, 128), F32),
            pltpu.VMEM((2, len(FAR), 8, 128), F32),
            dma((4,)),
            dma((2, 4)),
            dma((2, 4)),
            dma((2, 2)),
            dma((4,)),
            dma((4,)),
            dma((2,)),
            dma((3, 2)),
            dma((3, 2)),
            dma((3, 2, len(CUBE))),
            dma((3, 2, len(CUBE))),
            dma((2, len(FAR))),
            dma((2, len(FAR))),
            pltpu.SemaphoreType.REGULAR((len(RELAY),)),
        ],
        compiler_params=pltpu.CompilerParams(collective_id=0, has_side_effects=True, vmem_limit_bytes=56 * 2**20),
        name="block",
    )(tok, cot, wqkv, wout)


def body(tokens, cotangent, w_qkv, w_out):
    count = tokens.shape[0] * tokens.shape[1] * tokens.shape[2] * lax.axis_size("lon") * lax.axis_size("lat")
    grad_tokens, grad_qkv, grad_out = block(tokens, cotangent, w_qkv, w_out, 1.0 / math.sqrt(count))
    return grad_tokens, grad_qkv.reshape(-1), grad_out.reshape(-1)


def solution(mesh):
    in_specs = (P("lon", "lat", None, None), P("lon", "lat", None, None), P(), P())
    out_specs = (P("lon", "lat", None, None), P(("lon", "lat")), P(("lon", "lat")))
    return jax.shard_map(body, mesh=mesh, in_specs=in_specs, out_specs=out_specs, check_vma=False)
```

```python
import functools
import math

import jax
import jax.numpy as jnp
from jax import lax
from jax.experimental import pallas as pl
from jax.experimental.pallas import tpu as pltpu
from jax.sharding import PartitionSpec as P

D = 512
H = 16
E = 32
WIN = 144
SLAB = 2 * WIN
TOK = 2 * SLAB
GROUP = 8
LANES = GROUP * WIN
SCALE = 1.0 / math.sqrt(E)
BF = jnp.bfloat16
F32 = jnp.float32
MESH = pl.DeviceIdType.MESH
NN = (((1,), (0,)), ((), ()))
NT = (((1,), (1,)), ((), ()))
TN = (((0,), (0,)), ((), ()))


def mm(a, b, dims=NN):
    return lax.dot_general(a, b, dims, preferred_element_type=F32)


def near(lon, lat):
    n_lon, n_lat = lax.axis_size("lon"), lax.axis_size("lat")
    return ((lax.axis_index("lon") + lon + n_lon) % n_lon, (lax.axis_index("lat") + lat + n_lat) % n_lat)


HALO = ((0, 1), (0, -1), (1, 0), (-1, 0), (1, -1), (-1, 1))
SIZES = {"x": 4, "y": 8, "z": 8}
CUBE = tuple((a, b, c) for a in (1, 0) for b in (1, 0) for c in (1, 0) if a + b + c)
FAR = tuple((a, b, c) for a in (1, 0) for b in (2, 1, 3, 0) for c in (2, 1, 3, 0) if a + b + c)
RELAY = (("y", (2, -2)), ("z", (2, -2)), ("z", (2, -2)), ("x", (2,)))
PARTS = (((0, 2), (2, 4)), ((4, 8), (8, 12)), ((12, 14), (14, 16)))
QKV_BLOCKS = (4, 5, 12, 13, 6, 7, 14, 15, 8, 9, 10, 11)


def position():
    lon, lat = lax.axis_index("lon"), lax.axis_index("lat")
    return {"x": lon // 16, "y": lon % 8, "z": (lat // 2) * 2 + (lon // 8) % 2, "core": lat % 2}


def device(at):
    return (at["x"] * 16 + (at["z"] % 2) * 8 + at["y"], (at["z"] // 2) * 2 + at["core"])


def moved(at, **steps):
    new = dict(at)
    for axis, step in steps.items():
        size = SIZES.get(axis, 2)
        new[axis] = (at[axis] + step + size) % size
    return device(new)


def lane_head():
    return lax.broadcasted_iota(jnp.int32, (WIN, 256), 1) // E


def stack_heads(x):
    lane = lane_head()
    zero = jnp.zeros_like(x)
    return jnp.concatenate([jnp.where(lane == h, x, zero) for h in range(GROUP)], axis=0)


def pick_heads(r):
    lane = lane_head()
    out = r[0:WIN]
    for h in range(1, GROUP):
        out = jnp.where(lane == h, r[h * WIN : (h + 1) * WIN], out)
    return out


def level_order(rows, natural):
    return natural == 4 * (rows % 72) + (rows // 72 + 1) % 4


def owner_order(i, p):
    x = 2 * ((p // 16) % 2) + (p // 128) % 2
    y = 2 * ((p // 4) % 4) + (p // 64) % 2
    return i == x * 128 + ((p // 32) % 2) * 64 + y * 8 + (p % 4) * 2 + p // 256


def one_hot(relation, shape, swap=False):
    a = lax.broadcasted_iota(jnp.int32, shape, 1 if swap else 0)
    b = lax.broadcasted_iota(jnp.int32, shape, 0 if swap else 1)
    return jnp.where(relation(a, b), 1.0, 0.0).astype(BF)


def region(pos, split_level, split_lat):
    return (pos // 72) * split_level + 2 * split_lat * ((pos % 6) // 3)


def signal(sem, to):
    pl.semaphore_signal(sem, inc=1, device_id=to, device_id_type=MESH)


def remote(src, dst, send, recv, to):
    copy = pltpu.make_async_remote_copy(
        src_ref=src, dst_ref=dst, send_sem=send, recv_sem=recv, device_id=to, device_id_type=MESH
    )
    copy.start()
    return copy


def local(src, dst, sem):
    copy = pltpu.make_async_copy(src, dst, sem)
    copy.start()
    return copy


def block_kernel(norm, tok, cot, wqkv_in, wout_in, grad_tok, grad_qkv, grad_out, *scratch):
    (wqkv, wout, CT, own_path, ET, EC, X, XO, C, PR, A, DM, DA, DP, PT, path, G, R0, CB, RC, F, Q) = scratch[:22]
    (ws, hs, hr, hl, bs, br, bl, s0, r0, sc, rc, sf, rf, relay) = scratch[22:]
    at = position()
    bit = {axis: at[axis] % 2 for axis in SIZES}
    core = at["core"]
    lat = lax.axis_index("lat")
    last = lax.axis_size("lat") - 1

    greeted = [near(*step) for step in HALO] + [moved(at, core=1)]
    for a, b, c in CUBE:
        for sense in (1, -1):
            steps = {axis: sense * far * (1 - 2 * bit[axis]) for axis, far in (("x", a), ("y", b), ("z", c))}
            greeted.append(moved(at, **steps))
    greeted += [moved(at, **{axis: step}) for axis, steps in RELAY[1:] + RELAY[:1] for step in steps][2:]
    barrier = pltpu.get_barrier_semaphore()
    for other in greeted:
        signal(barrier, other)
    own = [local(wqkv_in, wqkv, ws.at[0]), local(wout_in, wout, ws.at[1]), local(cot, CT, ws.at[2])]
    pl.semaphore_wait(barrier, len(greeted))

    come = []
    for a, (src, ext) in enumerate(((tok, ET), (cot, EC))):
        come.append(
            (
                local(src.at[6:18, 3:6], ext.at[0, :, 0:3], hl.at[a, 0]),
                remote(src.at[6:18, 0:3], ext.at[0, :, 3:6], hs.at[a, 0], hr.at[a, 0], near(0, -1)),
            )
        )
        come.append(
            (
                local(src.at[18:24, 0:3], ext.at[1, 0:6, 3:6], hl.at[a, 1]),
                remote(src.at[18:24, 3:6], ext.at[1, 0:6, 0:3], hs.at[a, 1], hr.at[a, 1], near(0, 1)),
                remote(src.at[0:6, 3:6], ext.at[1, 6:12, 0:3], hs.at[a, 2], hr.at[a, 2], near(-1, 1)),
                remote(src.at[0:6, 0:3], ext.at[1, 6:12, 3:6], hs.at[a, 3], hr.at[a, 3], near(-1, 0)),
            )
        )

    def relay_send(n):
        axis, steps = RELAY[n]
        for step in steps:
            signal(relay.at[n], moved(at, **{axis: step}))

    def relay_wait(n):
        pl.semaphore_wait(relay.at[n], len(RELAY[n][1]))

    relay_send(0)
    own[0].wait()
    order = one_hot(level_order, (SLAB, SLAB))
    owner = one_hot(owner_order, (D, D), swap=True)

    def parts(rows, g):
        return [PR[rows, c * D + g * 256 : c * D + (g + 1) * 256] for c in range(3)]

    def forward(i):
        rows = pl.ds(i * WIN, WIN)
        split_lat = jnp.where(lat == (last if i < 2 else 0), 1, 0)
        key_region = region(lax.broadcasted_iota(jnp.int32, (WIN, 128), 0), i % 2, split_lat)
        for g in range(2):
            q, k, v = parts(rows, g)
            scores = mm(k, stack_heads(q), NT)
            probs_b = []
            for c in range(LANES // 128):
                cols = slice(c * 128, (c + 1) * 128)
                pos = lax.broadcasted_iota(jnp.int32, (1, 128), 1) + c * 128
                allowed = key_region == region(pos % WIN, i % 2, split_lat)
                s = jnp.where(allowed, scores[:, cols] * SCALE, -1e30)
                e = jnp.exp(s - jnp.max(s, axis=0, keepdims=True))
                p = e * (1.0 / jnp.sum(e, axis=0, keepdims=True))
                PT[i * 2 + g, :, cols] = p
                probs_b.append(p.astype(BF))
            probs_b = jnp.concatenate(probs_b, axis=1)
            A[rows, g * 256 : (g + 1) * 256] = pick_heads(mm(probs_b, v, TN)).astype(BF)

    for w in range(2):
        for copy in come[w]:
            copy.wait()
        rows = pl.ds(w * SLAB, SLAB)
        X[rows, :] = mm(order, ET[w].reshape(SLAB, D)).astype(BF)
        for c in range(3):
            cols = pl.ds(c * D, D)
            PR[rows, cols] = mm(X[rows, :], wqkv[:, cols]).astype(BF)
        for i in range(2 * w, 2 * w + 2):
            forward(i)
        relay_wait(w)
        relay_send(w + 1)

    XO[...] = mm(owner, X[...], NT).astype(BF)
    own[1].wait()
    for w in range(2):
        for copy in come[2 + w]:
            copy.wait()
        rows = pl.ds(w * SLAB, SLAB)
        C[rows, :] = mm(order, EC[w].reshape(SLAB, D)).astype(BF)
    for i in range(4):
        rows = pl.ds(i * WIN, WIN)
        mixed = mm(A[rows, :], wout[...])
        centred = mixed - jnp.mean(mixed, axis=-1, keepdims=True)
        rstd = lax.rsqrt(jnp.mean(centred * centred, axis=-1, keepdims=True) + 1e-5)
        normed = centred * rstd
        up = C[rows, :].astype(F32)
        d_mixed = rstd * (
            up - jnp.mean(up, axis=-1, keepdims=True) - normed * jnp.mean(up * normed, axis=-1, keepdims=True)
        )
        d_mixed = d_mixed.astype(BF)
        DM[rows, :] = d_mixed
        DA[rows, :] = mm(d_mixed, wout[...], NT).astype(BF)

    sent = []

    def span(lo, hi):
        return pl.ds(lo * 128, (hi - lo) * 128)

    def to_core(part):
        return [
            remote(
                G.at[1 - core, :, :, :, :, span(lo, hi)],
                R0.at[:, :, :, :, span(lo, hi)],
                s0.at[part, n],
                r0.at[part, n],
                moved(at, core=1),
            )
            for n, (lo, hi) in enumerate(PARTS[part])
        ]

    def to_cube(part, flying):
        out = []
        for n, (lo, hi) in enumerate(PARTS[part]):
            flying[n].wait_recv()
            sent.append(flying[n])
            cols = span(lo, hi)
            CB[:, :, :, :, cols] = (G[core, :, :, :, :, cols] + R0[:, :, :, :, cols]).astype(BF)
            for k, (a, b, c) in enumerate(CUBE):
                steps = {
                    axis: far * (1 - 2 * n) * (1 - 2 * bit[axis]) for axis, far in (("x", a), ("y", b), ("z", c)) if far
                }
                place = [1 - bit[axis] if far else bit[axis] for axis, far in (("x", a), ("y", b), ("z", c))]
                out.append(
                    remote(
                        CB.at[place[0], place[1], place[2], :, cols],
                        RC.at[k, :, cols],
                        sc.at[part, n, k],
                        rc.at[part, n, k],
                        moved(at, **steps),
                    )
                )
        return out

    def take_cube(part, flying):
        for copy in flying:
            copy.wait_recv()
        sent.extend(flying)
        for c in range(PARTS[part][0][0], PARTS[part][1][1]):
            cols = span(c, c + 1)
            value = G[core, bit["x"], bit["y"], bit["z"], :, cols] + R0[bit["x"], bit["y"], bit["z"], :, cols]
            for k in range(len(CUBE)):
                value = value + RC[k, :, cols].astype(F32)
            F[c // 8, pl.ds(c % 8, 32, stride=8), :] = value

    def row(a, b, c):
        place = ((at["x"] // 2 + a) % 2) * 16 + ((at["y"] // 2 + b) % 4) * 4 + (at["z"] // 2 + c) % 4
        return pl.ds(pl.multiple_of(place * 8, 8), 8)

    def to_far(half):
        return [
            remote(
                F.at[half, row(a, b, c)],
                Q.at[half, n],
                sf.at[half, n],
                rf.at[half, n],
                moved(at, x=2 * a, y=2 * b, z=2 * c),
            )
            for n, (a, b, c) in enumerate(FAR)
        ]

    def take_far(half, flying):
        value = F[half, row(0, 0, 0), :]
        for n, copy in enumerate(flying):
            copy.wait_recv()
            value = value + Q[half, n]
        sent.extend(flying)
        return value * norm

    def backward(g, i):
        rows = pl.ds(i * WIN, WIN)
        q, k, v = parts(rows, g)
        d_att = stack_heads(DA[rows, g * 256 : (g + 1) * 256])
        d_probs = mm(v, d_att, NT)
        probs_b, d_scores = [], []
        for c in range(LANES // 128):
            cols = slice(c * 128, (c + 1) * 128)
            p = PT[i * 2 + g, :, cols]
            dp = d_probs[:, cols]
            probs_b.append(p.astype(BF))
            d_scores.append((p * (dp - jnp.sum(dp * p, axis=0, keepdims=True)) * SCALE).astype(BF))
        d_scores = jnp.concatenate(d_scores, axis=1)
        for c, part in enumerate((pick_heads(mm(d_scores, k, TN)), mm(d_scores, stack_heads(q)))):
            DP[rows, c * D + g * 256 : c * D + (g + 1) * 256] = part.astype(BF)
        if g == 0:
            d_values = [mm(jnp.concatenate(probs_b, axis=1), d_att)]
            d_values.append(mm(PT[i * 2 + 1].astype(BF), stack_heads(DA[rows, 256:D])))
            DP[rows, 2 * D : 3 * D] = jnp.concatenate(d_values, axis=1).astype(BF)

    def weight_grad(block, lo, hi):
        G[:, :, :, :, :, span(block, block + (hi - lo) // 128)] = mm(XO[...], DP[:, lo:hi]).reshape(
            2, 2, 2, 2, 32, hi - lo
        )

    G[:, :, :, :, :, 0:D] = mm(mm(owner, A[...], NT).astype(BF), DM[...]).reshape(2, 2, 2, 2, 32, D)
    core_out = to_core(0)
    relay_wait(2)
    relay_send(3)
    for i in range(4):
        backward(0, i)
    cube_out = to_cube(0, core_out)
    weight_grad(4, 0, 256)
    weight_grad(6, D, D + 256)
    weight_grad(8, 2 * D, 3 * D)
    core_first = to_core(1)
    relay_wait(3)
    for i in range(4):
        backward(1, i)
    weight_grad(12, 256, D)
    weight_grad(14, D + 256, 2 * D)
    core_second = to_core(2)
    cube_first = to_cube(1, core_first)

    back = one_hot(level_order, (SLAB, SLAB), swap=True)
    for w in range(2):
        grads = mm(DP[pl.ds(w * SLAB, SLAB), :], wqkv[...], NT).astype(BF)
        path[w] = mm(back, grads).astype(BF).reshape(path.shape[1:])
    cube_second = to_cube(2, core_second)
    take_cube(0, cube_out)
    backs = [
        remote(path.at[0, :, 3:6], own_path.at[6:18, 0:3], bs.at[0], br.at[0], near(0, 1)),
        remote(path.at[1, 0:6, 0:3], own_path.at[18:24, 3:6], bs.at[1], br.at[1], near(0, -1)),
        remote(path.at[1, 6:12, 0:3], own_path.at[0:6, 3:6], bs.at[2], br.at[2], near(1, -1)),
        remote(path.at[1, 6:12, 3:6], own_path.at[0:6, 0:3], bs.at[3], br.at[3], near(1, 0)),
        local(path.at[0, :, 0:3], own_path.at[6:18, 3:6], bl.at[0]),
        local(path.at[1, 0:6, 3:6], own_path.at[18:24, 0:3], bl.at[1]),
    ]
    take_cube(1, cube_first)
    far_first = to_far(0)
    take_cube(2, cube_second)
    far_second = to_far(1)
    for copy in backs:
        copy.wait()
    own[2].wait()

    def add(i, _):
        CT[i] = (CT[i].astype(F32) + own_path[i].astype(F32)).astype(BF)
        return 0

    lax.fori_loop(0, CT.shape[0], add, 0)
    out = local(CT, grad_tok, ws.at[3])
    low = take_far(0, far_first)
    high = take_far(1, far_second)
    grad_out[...] = low[0:4]
    for n, block in enumerate(QKV_BLOCKS):
        grad_qkv[n : n + 1, :] = (low, high)[block // 8][block % 8 : block % 8 + 1]
    for copy in sent:
        copy.wait_send()
    out.wait()


def block(tok, cot, wqkv, wout, norm):
    vm = pl.BlockSpec(memory_space=pltpu.VMEM)
    any_ = pl.BlockSpec(memory_space=pl.ANY)
    rows = pltpu.VMEM((TOK, D), BF)
    wide = pltpu.VMEM((TOK, 3 * D), BF)
    ext = pltpu.VMEM((2, 12, 6, 4, D), BF)
    dma = pltpu.SemaphoreType.DMA
    return pl.pallas_call(
        functools.partial(block_kernel, norm),
        out_shape=(
            jax.ShapeDtypeStruct(tok.shape, BF),
            jax.ShapeDtypeStruct((12, 128), F32),
            jax.ShapeDtypeStruct((4, 128), F32),
        ),
        in_specs=[any_] * 4,
        out_specs=(any_, vm, vm),
        scratch_shapes=[
            pltpu.VMEM(wqkv.shape, BF),
            pltpu.VMEM(wout.shape, BF),
            pltpu.VMEM(tok.shape, BF),
            pltpu.VMEM(tok.shape, BF),
            ext,
            ext,
            rows,
            pltpu.VMEM((D, TOK), BF),
            rows,
            wide,
            rows,
            rows,
            rows,
            wide,
            pltpu.VMEM((8, WIN, LANES), F32),
            ext,
            pltpu.VMEM((2, 2, 2, 2, 32, 4 * D), F32),
            pltpu.VMEM((2, 2, 2, 32, 4 * D), F32),
            pltpu.VMEM((2, 2, 2, 32, 4 * D), BF),
            pltpu.VMEM((len(CUBE), 32, 4 * D), BF),
            pltpu.VMEM((2, 32 * 8, 128), F32),
            pltpu.VMEM((2, len(FAR), 8, 128), F32),
            dma((4,)),
            dma((2, 4)),
            dma((2, 4)),
            dma((2, 2)),
            dma((4,)),
            dma((4,)),
            dma((2,)),
            dma((3, 2)),
            dma((3, 2)),
            dma((3, 2, len(CUBE))),
            dma((3, 2, len(CUBE))),
            dma((2, len(FAR))),
            dma((2, len(FAR))),
            pltpu.SemaphoreType.REGULAR((len(RELAY),)),
        ],
        compiler_params=pltpu.CompilerParams(collective_id=0, has_side_effects=True, vmem_limit_bytes=56 * 2**20),
        name="block",
    )(tok, cot, wqkv, wout)


def body(tokens, cotangent, w_qkv, w_out):
    count = tokens.shape[0] * tokens.shape[1] * tokens.shape[2] * lax.axis_size("lon") * lax.axis_size("lat")
    grad_tokens, grad_qkv, grad_out = block(tokens, cotangent, w_qkv, w_out, 1.0 / math.sqrt(count))
    return grad_tokens, grad_qkv.reshape(-1), grad_out.reshape(-1)


def solution(mesh):
    in_specs = (P("lon", "lat", None, None), P("lon", "lat", None, None), P(), P())
    out_specs = (P("lon", "lat", None, None), P(("lon", "lat")), P(("lon", "lat")))
    return jax.shard_map(body, mesh=mesh, in_specs=in_specs, out_specs=out_specs, check_vma=False)
```

```python
import functools
import math

import jax
import jax.numpy as jnp
from jax import lax
from jax.experimental import pallas as pl
from jax.experimental.pallas import tpu as pltpu
from jax.sharding import PartitionSpec as P

D = 512
H = 16
E = 32
WIN = 144
SLAB = 2 * WIN
TOK = 2 * SLAB
GROUP = 8
LANES = GROUP * WIN
SCALE = 1.0 / math.sqrt(E)
BF = jnp.bfloat16
F32 = jnp.float32
MESH = pl.DeviceIdType.MESH
NN = (((1,), (0,)), ((), ()))
NT = (((1,), (1,)), ((), ()))
TN = (((0,), (0,)), ((), ()))


def mm(a, b, dims=NN):
    return lax.dot_general(a, b, dims, preferred_element_type=F32)


def near(lon, lat):
    n_lon, n_lat = lax.axis_size("lon"), lax.axis_size("lat")
    return ((lax.axis_index("lon") + lon + n_lon) % n_lon, (lax.axis_index("lat") + lat + n_lat) % n_lat)


HALO = ((0, 1), (0, -1), (1, 0), (-1, 0), (1, -1), (-1, 1))
SIZES = {"x": 4, "y": 8, "z": 8}
CUBE = tuple((a, b, c) for a in (1, 0) for b in (1, 0) for c in (1, 0) if a + b + c)
FAR = tuple((a, b, c) for a in (1, 0) for b in (2, 1, 3, 0) for c in (2, 1, 3, 0) if a + b + c)
RELAY = (("y", (2, -2)), ("z", (2, -2)), ("z", (2, -2)), ("x", (2,)))
PARTS = (((0, 2), (2, 4)), ((4, 6), (6, 8)), ((8, 10), (10, 12)), ((12, 14), (14, 16)))
QKV_BLOCKS = (8, 9, 12, 13, 10, 11, 14, 15, 4, 5, 6, 7)


def position():
    lon, lat = lax.axis_index("lon"), lax.axis_index("lat")
    return {"x": lon // 16, "y": lon % 8, "z": (lat // 2) * 2 + (lon // 8) % 2, "core": lat % 2}


def device(at):
    return (at["x"] * 16 + (at["z"] % 2) * 8 + at["y"], (at["z"] // 2) * 2 + at["core"])


def moved(at, **steps):
    new = dict(at)
    for axis, step in steps.items():
        size = SIZES.get(axis, 2)
        new[axis] = (at[axis] + step + size) % size
    return device(new)


def lane_head():
    return lax.broadcasted_iota(jnp.int32, (WIN, 256), 1) // E


def stack_heads(x):
    lane = lane_head()
    zero = jnp.zeros_like(x)
    return jnp.concatenate([jnp.where(lane == h, x, zero) for h in range(GROUP)], axis=0)


def pick_heads(r):
    lane = lane_head()
    out = r[0:WIN]
    for h in range(1, GROUP):
        out = jnp.where(lane == h, r[h * WIN : (h + 1) * WIN], out)
    return out


def level_order(rows, natural):
    return natural == 4 * (rows % 72) + (rows // 72 + 1) % 4


def owner_order(i, p):
    x = 2 * ((p // 16) % 2) + (p // 128) % 2
    y = 2 * ((p // 4) % 4) + (p // 64) % 2
    return i == x * 128 + ((p // 32) % 2) * 64 + y * 8 + (p % 4) * 2 + p // 256


def one_hot(relation, shape, swap=False):
    a = lax.broadcasted_iota(jnp.int32, shape, 1 if swap else 0)
    b = lax.broadcasted_iota(jnp.int32, shape, 0 if swap else 1)
    return jnp.where(relation(a, b), 1.0, 0.0).astype(BF)


def region(pos, split_level, split_lat):
    return (pos // 72) * split_level + 2 * split_lat * ((pos % 6) // 3)


def signal(sem, to):
    pl.semaphore_signal(sem, inc=1, device_id=to, device_id_type=MESH)


def remote(src, dst, send, recv, to):
    copy = pltpu.make_async_remote_copy(
        src_ref=src, dst_ref=dst, send_sem=send, recv_sem=recv, device_id=to, device_id_type=MESH
    )
    copy.start()
    return copy


def local(src, dst, sem):
    copy = pltpu.make_async_copy(src, dst, sem)
    copy.start()
    return copy


def block_kernel(norm, tok, cot, wqkv_in, wout_in, grad_tok, grad_qkv, grad_out, *scratch):
    (wqkv, wout, CT, own_path, ET, EC, X, XO, C, PR, A, DM, DA, DP, PT, path, G, R0, CB, RC, F, F2, F3, Q, Q2, Q3) = scratch[:26]
    (ws, hs, hr, hl, bs, br, bl, s0, r0, sc, rc, sf, rf, relay) = scratch[26:]
    at = position()
    bit = {axis: at[axis] % 2 for axis in SIZES}
    core = at["core"]
    lat = lax.axis_index("lat")
    last = lax.axis_size("lat") - 1

    greeted = [near(*step) for step in HALO] + [moved(at, core=1)]
    for a, b, c in CUBE:
        for sense in (1, -1):
            steps = {axis: sense * far * (1 - 2 * bit[axis]) for axis, far in (("x", a), ("y", b), ("z", c))}
            greeted.append(moved(at, **steps))
    greeted += [moved(at, **{axis: step}) for axis, steps in RELAY[1:] + RELAY[:1] for step in steps][2:]
    barrier = pltpu.get_barrier_semaphore()
    for other in greeted:
        signal(barrier, other)
    own = [local(wqkv_in, wqkv, ws.at[0]), local(wout_in, wout, ws.at[1]), local(cot, CT, ws.at[2])]
    pl.semaphore_wait(barrier, len(greeted))

    come = []
    for a, (src, ext) in enumerate(((tok, ET), (cot, EC))):
        come.append(
            (
                local(src.at[6:18, 3:6], ext.at[0, :, 0:3], hl.at[a, 0]),
                remote(src.at[6:18, 0:3], ext.at[0, :, 3:6], hs.at[a, 0], hr.at[a, 0], near(0, -1)),
            )
        )
        come.append(
            (
                local(src.at[18:24, 0:3], ext.at[1, 0:6, 3:6], hl.at[a, 1]),
                remote(src.at[18:24, 3:6], ext.at[1, 0:6, 0:3], hs.at[a, 1], hr.at[a, 1], near(0, 1)),
                remote(src.at[0:6, 3:6], ext.at[1, 6:12, 0:3], hs.at[a, 2], hr.at[a, 2], near(-1, 1)),
                remote(src.at[0:6, 0:3], ext.at[1, 6:12, 3:6], hs.at[a, 3], hr.at[a, 3], near(-1, 0)),
            )
        )

    def relay_send(n):
        axis, steps = RELAY[n]
        for step in steps:
            signal(relay.at[n], moved(at, **{axis: step}))

    def relay_wait(n):
        pl.semaphore_wait(relay.at[n], len(RELAY[n][1]))

    relay_send(0)
    own[0].wait()
    order = one_hot(level_order, (SLAB, SLAB))
    owner = one_hot(owner_order, (D, D), swap=True)

    def parts(rows, g):
        return [PR[rows, c * D + g * 256 : c * D + (g + 1) * 256] for c in range(3)]

    def forward(i):
        rows = pl.ds(i * WIN, WIN)
        split_lat = jnp.where(lat == (last if i < 2 else 0), 1, 0)
        key_region = region(lax.broadcasted_iota(jnp.int32, (WIN, 128), 0), i % 2, split_lat)
        for g in range(2):
            q, k, v = parts(rows, g)
            scores = mm(k, stack_heads(q), NT)
            probs_b = []
            for c in range(LANES // 128):
                cols = slice(c * 128, (c + 1) * 128)
                pos = lax.broadcasted_iota(jnp.int32, (1, 128), 1) + c * 128
                allowed = key_region == region(pos % WIN, i % 2, split_lat)
                s = jnp.where(allowed, scores[:, cols] * SCALE, -1e30)
                e = jnp.exp(s - jnp.max(s, axis=0, keepdims=True))
                p = e * (1.0 / jnp.sum(e, axis=0, keepdims=True))
                PT[i * 2 + g, :, cols] = p
                probs_b.append(p.astype(BF))
            probs_b = jnp.concatenate(probs_b, axis=1)
            A[rows, g * 256 : (g + 1) * 256] = pick_heads(mm(probs_b, v, TN)).astype(BF)

    for w in range(2):
        for copy in come[w]:
            copy.wait()
        rows = pl.ds(w * SLAB, SLAB)
        X[rows, :] = mm(order, ET[w].reshape(SLAB, D)).astype(BF)
        for c in range(3):
            cols = pl.ds(c * D, D)
            PR[rows, cols] = mm(X[rows, :], wqkv[:, cols]).astype(BF)
        for i in range(2 * w, 2 * w + 2):
            forward(i)
        relay_wait(w)
        relay_send(w + 1)

    XO[...] = mm(owner, X[...], NT).astype(BF)
    own[1].wait()
    for w in range(2):
        for copy in come[2 + w]:
            copy.wait()
        rows = pl.ds(w * SLAB, SLAB)
        C[rows, :] = mm(order, EC[w].reshape(SLAB, D)).astype(BF)
    for i in range(4):
        rows = pl.ds(i * WIN, WIN)
        mixed = mm(A[rows, :], wout[...])
        centred = mixed - jnp.mean(mixed, axis=-1, keepdims=True)
        rstd = lax.rsqrt(jnp.mean(centred * centred, axis=-1, keepdims=True) + 1e-5)
        normed = centred * rstd
        up = C[rows, :].astype(F32)
        d_mixed = rstd * (
            up - jnp.mean(up, axis=-1, keepdims=True) - normed * jnp.mean(up * normed, axis=-1, keepdims=True)
        )
        d_mixed = d_mixed.astype(BF)
        DM[rows, :] = d_mixed
        DA[rows, :] = mm(d_mixed, wout[...], NT).astype(BF)

    sent = []
    rows_of = (F, F, F2, F3)

    def span(lo, hi):
        return pl.ds(lo * 128, (hi - lo) * 128)

    def to_core(part):
        return [
            remote(
                G.at[1 - core, :, :, :, :, span(lo, hi)],
                R0.at[:, :, :, :, span(lo, hi)],
                s0.at[part, n],
                r0.at[part, n],
                moved(at, core=1),
            )
            for n, (lo, hi) in enumerate(PARTS[part])
        ]

    def to_cube(part, flying):
        out = []
        for n, (lo, hi) in enumerate(PARTS[part]):
            flying[n].wait_recv()
            sent.append(flying[n])
            cols = span(lo, hi)
            CB[:, :, :, :, cols] = (G[core, :, :, :, :, cols] + R0[:, :, :, :, cols]).astype(BF)
            for k, (a, b, c) in enumerate(CUBE):
                steps = {
                    axis: far * (1 - 2 * n) * (1 - 2 * bit[axis]) for axis, far in (("x", a), ("y", b), ("z", c)) if far
                }
                place = [1 - bit[axis] if far else bit[axis] for axis, far in (("x", a), ("y", b), ("z", c))]
                out.append(
                    remote(
                        CB.at[place[0], place[1], place[2], :, cols],
                        RC.at[k, :, cols],
                        sc.at[part, n, k],
                        rc.at[part, n, k],
                        moved(at, **steps),
                    )
                )
        return out

    def take_cube(part, flying):
        for copy in flying:
            copy.wait_recv()
        sent.extend(flying)
        for c in range(PARTS[part][0][0], PARTS[part][1][1]):
            cols = span(c, c + 1)
            value = G[core, bit["x"], bit["y"], bit["z"], :, cols] + R0[bit["x"], bit["y"], bit["z"], :, cols]
            for k in range(len(CUBE)):
                value = value + RC[k, :, cols].astype(F32)
            rows_of[c // 4][:, c if c < 8 else c % 4, :] = value

    def row(a, b, c):
        return ((at["x"] // 2 + a) % 2) * 16 + ((at["y"] // 2 + b) % 4) * 4 + (at["z"] // 2 + c) % 4

    def to_far(n, src, dst):
        return [
            remote(
                src.at[row(a, b, c)],
                dst.at[k],
                sf.at[n, k],
                rf.at[n, k],
                moved(at, x=2 * a, y=2 * b, z=2 * c),
            )
            for k, (a, b, c) in enumerate(FAR)
        ]

    def take_far(src, dst, flying):
        value = src[row(0, 0, 0)]
        for k, copy in enumerate(flying):
            copy.wait_recv()
            value = value + dst[k]
        sent.extend(flying)
        return value * norm

    def backward(g, i):
        rows = pl.ds(i * WIN, WIN)
        q, k, v = parts(rows, g)
        d_att = stack_heads(DA[rows, g * 256 : (g + 1) * 256])
        d_probs = mm(v, d_att, NT)
        d_scores = []
        for c in range(LANES // 128):
            cols = slice(c * 128, (c + 1) * 128)
            p = PT[i * 2 + g, :, cols]
            dp = d_probs[:, cols]
            d_scores.append((p * (dp - jnp.sum(dp * p, axis=0, keepdims=True)) * SCALE).astype(BF))
        d_scores = jnp.concatenate(d_scores, axis=1)
        for c, part in enumerate((pick_heads(mm(d_scores, k, TN)), mm(d_scores, stack_heads(q)))):
            DP[rows, c * D + g * 256 : c * D + (g + 1) * 256] = part.astype(BF)

    def values(g, i):
        rows = pl.ds(i * WIN, WIN)
        cols = slice(g * 256, (g + 1) * 256)
        DP[rows, 2 * D + g * 256 : 2 * D + (g + 1) * 256] = mm(
            PT[i * 2 + g].astype(BF), stack_heads(DA[rows, cols])
        ).astype(BF)

    def weight_grad(block, lo, hi):
        G[:, :, :, :, :, span(block, block + (hi - lo) // 128)] = mm(XO[...], DP[:, lo:hi]).reshape(
            2, 2, 2, 2, 32, hi - lo
        )

    G[:, :, :, :, :, 0:D] = mm(mm(owner, A[...], NT).astype(BF), DM[...]).reshape(2, 2, 2, 2, 32, D)
    core_0 = to_core(0)
    relay_wait(2)
    relay_send(3)
    for i in range(4):
        values(0, i)
        values(1, i)
    weight_grad(4, 2 * D, 3 * D)
    core_1 = to_core(1)
    for i in range(4):
        backward(0, i)
    cube_0 = to_cube(0, core_0)
    weight_grad(8, 0, 256)
    weight_grad(10, D, D + 256)
    core_2 = to_core(2)
    relay_wait(3)
    for i in range(4):
        backward(1, i)
    cube_1 = to_cube(1, core_1)
    weight_grad(12, 256, D)
    weight_grad(14, D + 256, 2 * D)
    core_3 = to_core(3)
    cube_2 = to_cube(2, core_2)

    back = one_hot(level_order, (SLAB, SLAB), swap=True)
    for w in range(2):
        grads = mm(DP[pl.ds(w * SLAB, SLAB), :], wqkv[...], NT).astype(BF)
        path[w] = mm(back, grads).astype(BF).reshape(path.shape[1:])
    cube_3 = to_cube(3, core_3)
    take_cube(0, cube_0)
    take_cube(1, cube_1)
    far_1 = to_far(0, F, Q)
    take_cube(2, cube_2)
    far_2 = to_far(1, F2, Q2)
    take_cube(3, cube_3)
    far_3 = to_far(2, F3, Q3)
    backs = [
        remote(path.at[0, :, 3:6], own_path.at[6:18, 0:3], bs.at[0], br.at[0], near(0, 1)),
        remote(path.at[1, 0:6, 0:3], own_path.at[18:24, 3:6], bs.at[1], br.at[1], near(0, -1)),
        remote(path.at[1, 6:12, 0:3], own_path.at[0:6, 3:6], bs.at[2], br.at[2], near(1, -1)),
        remote(path.at[1, 6:12, 3:6], own_path.at[0:6, 0:3], bs.at[3], br.at[3], near(1, 0)),
        local(path.at[0, :, 0:3], own_path.at[6:18, 3:6], bl.at[0]),
        local(path.at[1, 0:6, 3:6], own_path.at[18:24, 0:3], bl.at[1]),
    ]
    for copy in backs:
        copy.wait()
    own[2].wait()

    def add(i, _):
        CT[i] = (CT[i].astype(F32) + own_path[i].astype(F32)).astype(BF)
        return 0

    lax.fori_loop(0, CT.shape[0], add, 0)
    out = local(CT, grad_tok, ws.at[3])
    sums = jnp.concatenate([take_far(F, Q, far_1), take_far(F2, Q2, far_2), take_far(F3, Q3, far_3)], axis=0)
    grad_out[...] = sums[0:4]
    for n, c in enumerate(QKV_BLOCKS):
        grad_qkv[n : n + 1, :] = sums[c : c + 1]
    for copy in sent:
        copy.wait_send()
    out.wait()


def block(tok, cot, wqkv, wout, norm):
    vm = pl.BlockSpec(memory_space=pltpu.VMEM)
    any_ = pl.BlockSpec(memory_space=pl.ANY)
    rows = pltpu.VMEM((TOK, D), BF)
    wide = pltpu.VMEM((TOK, 3 * D), BF)
    ext = pltpu.VMEM((2, 12, 6, 4, D), BF)
    dma = pltpu.SemaphoreType.DMA
    return pl.pallas_call(
        functools.partial(block_kernel, norm),
        out_shape=(
            jax.ShapeDtypeStruct(tok.shape, BF),
            jax.ShapeDtypeStruct((12, 128), F32),
            jax.ShapeDtypeStruct((4, 128), F32),
        ),
        in_specs=[any_] * 4,
        out_specs=(any_, vm, vm),
        scratch_shapes=[
            pltpu.VMEM(wqkv.shape, BF),
            pltpu.VMEM(wout.shape, BF),
            pltpu.VMEM(tok.shape, BF),
            pltpu.VMEM(tok.shape, BF),
            ext,
            ext,
            rows,
            pltpu.VMEM((D, TOK), BF),
            rows,
            wide,
            rows,
            rows,
            rows,
            wide,
            pltpu.VMEM((8, WIN, LANES), F32),
            ext,
            pltpu.VMEM((2, 2, 2, 2, 32, 4 * D), F32),
            pltpu.VMEM((2, 2, 2, 32, 4 * D), F32),
            pltpu.VMEM((2, 2, 2, 32, 4 * D), BF),
            pltpu.VMEM((len(CUBE), 32, 4 * D), BF),
            *(pltpu.VMEM((32, n, 128), F32) for n in (8, 4, 4)),
            *(pltpu.VMEM((len(FAR), n, 128), F32) for n in (8, 4, 4)),
            dma((4,)),
            dma((2, 4)),
            dma((2, 4)),
            dma((2, 2)),
            dma((4,)),
            dma((4,)),
            dma((2,)),
            dma((4, 2)),
            dma((4, 2)),
            dma((4, 2, len(CUBE))),
            dma((4, 2, len(CUBE))),
            dma((3, len(FAR))),
            dma((3, len(FAR))),
            pltpu.SemaphoreType.REGULAR((len(RELAY),)),
        ],
        compiler_params=pltpu.CompilerParams(collective_id=0, has_side_effects=True, vmem_limit_bytes=56 * 2**20),
        name="block",
    )(tok, cot, wqkv, wout)


def body(tokens, cotangent, w_qkv, w_out):
    count = tokens.shape[0] * tokens.shape[1] * tokens.shape[2] * lax.axis_size("lon") * lax.axis_size("lat")
    grad_tokens, grad_qkv, grad_out = block(tokens, cotangent, w_qkv, w_out, 1.0 / math.sqrt(count))
    return grad_tokens, grad_qkv.reshape(-1), grad_out.reshape(-1)


def solution(mesh):
    in_specs = (P("lon", "lat", None, None), P("lon", "lat", None, None), P(), P())
    out_specs = (P("lon", "lat", None, None), P(("lon", "lat")), P(("lon", "lat")))
    return jax.shard_map(body, mesh=mesh, in_specs=in_specs, out_specs=out_specs, check_vma=False)
```

```python
import functools
import math

import jax
import jax.numpy as jnp
from jax import lax
from jax.experimental import pallas as pl
from jax.experimental.pallas import tpu as pltpu
from jax.sharding import PartitionSpec as P

D = 512
H = 16
E = 32
WIN = 144
SLAB = 2 * WIN
TOK = 2 * SLAB
GROUP = 8
LANES = GROUP * WIN
SCALE = 1.0 / math.sqrt(E)
BF = jnp.bfloat16
F32 = jnp.float32
MESH = pl.DeviceIdType.MESH
NN = (((1,), (0,)), ((), ()))
NT = (((1,), (1,)), ((), ()))
TN = (((0,), (0,)), ((), ()))


def mm(a, b, dims=NN):
    return lax.dot_general(a, b, dims, preferred_element_type=F32)


def near(lon, lat):
    n_lon, n_lat = lax.axis_size("lon"), lax.axis_size("lat")
    return ((lax.axis_index("lon") + lon + n_lon) % n_lon, (lax.axis_index("lat") + lat + n_lat) % n_lat)


HALO = ((0, 1), (0, -1), (1, 0), (-1, 0), (1, -1), (-1, 1))
SIZES = {"x": 4, "y": 8, "z": 8}
CUBE = tuple((a, b, c) for a in (1, 0) for b in (1, 0) for c in (1, 0) if a + b + c)
FAR = tuple((a, b, c) for a in (1, 0) for b in (2, 1, 3, 0) for c in (2, 1, 3, 0) if a + b + c)
RELAY = (("y", (2, -2)), ("z", (2, -2)), ("z", (2, -2)), ("x", (2,)))
PARTS = (((0, 2), (2, 4)), ((4, 8), (8, 12)), ((12, 14), (14, 16)))
QKV_BLOCKS = (4, 5, 12, 13, 6, 7, 14, 15, 8, 9, 10, 11)


def position():
    lon, lat = lax.axis_index("lon"), lax.axis_index("lat")
    return {"x": lon // 16, "y": lon % 8, "z": (lat // 2) * 2 + (lon // 8) % 2, "core": lat % 2}


def device(at):
    return (at["x"] * 16 + (at["z"] % 2) * 8 + at["y"], (at["z"] // 2) * 2 + at["core"])


def moved(at, **steps):
    new = dict(at)
    for axis, step in steps.items():
        size = SIZES.get(axis, 2)
        new[axis] = (at[axis] + step + size) % size
    return device(new)


def lane_head():
    return lax.broadcasted_iota(jnp.int32, (WIN, 256), 1) // E


def stack_heads(x):
    lane = lane_head()
    zero = jnp.zeros_like(x)
    return jnp.concatenate([jnp.where(lane == h, x, zero) for h in range(GROUP)], axis=0)


def pick_heads(r):
    lane = lane_head()
    out = r[0:WIN]
    for h in range(1, GROUP):
        out = jnp.where(lane == h, r[h * WIN : (h + 1) * WIN], out)
    return out


def level_order(rows, natural):
    return natural == 4 * (rows % 72) + (rows // 72 + 1) % 4


def owner_order(i, p):
    x = 2 * ((p // 16) % 2) + (p // 128) % 2
    y = 2 * ((p // 4) % 4) + (p // 64) % 2
    return i == x * 128 + ((p // 32) % 2) * 64 + y * 8 + (p % 4) * 2 + p // 256


def one_hot(relation, shape, swap=False):
    a = lax.broadcasted_iota(jnp.int32, shape, 1 if swap else 0)
    b = lax.broadcasted_iota(jnp.int32, shape, 0 if swap else 1)
    return jnp.where(relation(a, b), 1.0, 0.0).astype(BF)


def region(pos, split_level, split_lat):
    return (pos // 72) * split_level + 2 * split_lat * ((pos % 6) // 3)


def signal(sem, to):
    pl.semaphore_signal(sem, inc=1, device_id=to, device_id_type=MESH)


def remote(src, dst, send, recv, to):
    copy = pltpu.make_async_remote_copy(
        src_ref=src, dst_ref=dst, send_sem=send, recv_sem=recv, device_id=to, device_id_type=MESH
    )
    copy.start()
    return copy


def local(src, dst, sem):
    copy = pltpu.make_async_copy(src, dst, sem)
    copy.start()
    return copy


def block_kernel(norm, tok, cot, wqkv_in, wout_in, grad_tok, grad_qkv, grad_out, *scratch):
    (wqkv, wout, CT, own_path, ET, EC, X, XO, C, PR, A, DM, DA, DP, PT, path, G, R0, CB, RC, F, Q) = scratch[:22]
    (ws, hs, hr, hl, bs, br, bl, s0, r0, sc, rc, sf, rf, relay) = scratch[22:]
    at = position()
    bit = {axis: at[axis] % 2 for axis in SIZES}
    core = at["core"]
    lat = lax.axis_index("lat")
    last = lax.axis_size("lat") - 1

    greeted = [near(*step) for step in HALO] + [moved(at, core=1)]
    for a, b, c in CUBE:
        for sense in (1, -1):
            steps = {axis: sense * far * (1 - 2 * bit[axis]) for axis, far in (("x", a), ("y", b), ("z", c))}
            greeted.append(moved(at, **steps))
    greeted += [moved(at, **{axis: step}) for axis, steps in RELAY[1:] + RELAY[:1] for step in steps][2:]
    barrier = pltpu.get_barrier_semaphore()
    for other in greeted:
        signal(barrier, other)
    own = [local(wqkv_in, wqkv, ws.at[0]), local(wout_in, wout, ws.at[1]), local(cot, CT, ws.at[2])]
    pl.semaphore_wait(barrier, len(greeted))

    come = []
    for a, (src, ext) in enumerate(((tok, ET), (cot, EC))):
        come.append(
            (
                local(src.at[6:18, 3:6], ext.at[0, :, 0:3], hl.at[a, 0]),
                remote(src.at[6:18, 0:3], ext.at[0, :, 3:6], hs.at[a, 0], hr.at[a, 0], near(0, -1)),
            )
        )
        come.append(
            (
                local(src.at[18:24, 0:3], ext.at[1, 0:6, 3:6], hl.at[a, 1]),
                remote(src.at[18:24, 3:6], ext.at[1, 0:6, 0:3], hs.at[a, 1], hr.at[a, 1], near(0, 1)),
                remote(src.at[0:6, 3:6], ext.at[1, 6:12, 0:3], hs.at[a, 2], hr.at[a, 2], near(-1, 1)),
                remote(src.at[0:6, 0:3], ext.at[1, 6:12, 3:6], hs.at[a, 3], hr.at[a, 3], near(-1, 0)),
            )
        )

    def relay_send(n):
        axis, steps = RELAY[n]
        for step in steps:
            signal(relay.at[n], moved(at, **{axis: step}))

    def relay_wait(n):
        pl.semaphore_wait(relay.at[n], len(RELAY[n][1]))

    relay_send(0)
    own[0].wait()
    order = one_hot(level_order, (SLAB, SLAB))
    owner = one_hot(owner_order, (D, D), swap=True)

    def parts(rows, g):
        return [PR[rows, c * D + g * 256 : c * D + (g + 1) * 256] for c in range(3)]

    def forward(i):
        rows = pl.ds(i * WIN, WIN)
        split_lat = jnp.where(lat == (last if i < 2 else 0), 1, 0)
        key_region = region(lax.broadcasted_iota(jnp.int32, (WIN, 128), 0), i % 2, split_lat)
        for g in range(2):
            q, k, v = parts(rows, g)
            scores = mm(k, stack_heads(q), NT)
            probs_b = []
            for c in range(LANES // 128):
                cols = slice(c * 128, (c + 1) * 128)
                pos = lax.broadcasted_iota(jnp.int32, (1, 128), 1) + c * 128
                allowed = key_region == region(pos % WIN, i % 2, split_lat)
                s = jnp.where(allowed, scores[:, cols] * SCALE, -1e30)
                e = jnp.exp(s - jnp.max(s, axis=0, keepdims=True))
                p = e * (1.0 / jnp.sum(e, axis=0, keepdims=True))
                PT[i * 2 + g, :, cols] = p
                probs_b.append(p.astype(BF))
            probs_b = jnp.concatenate(probs_b, axis=1)
            A[rows, g * 256 : (g + 1) * 256] = pick_heads(mm(probs_b, v, TN)).astype(BF)

    for w in range(2):
        for copy in come[w]:
            copy.wait()
        rows = pl.ds(w * SLAB, SLAB)
        X[rows, :] = mm(order, ET[w].reshape(SLAB, D)).astype(BF)
        for c in range(3):
            cols = pl.ds(c * D, D)
            PR[rows, cols] = mm(X[rows, :], wqkv[:, cols]).astype(BF)
        for i in range(2 * w, 2 * w + 2):
            forward(i)
        relay_wait(w)
        relay_send(w + 1)

    XO[...] = mm(owner, X[...], NT).astype(BF)
    own[1].wait()
    for w in range(2):
        for copy in come[2 + w]:
            copy.wait()
        rows = pl.ds(w * SLAB, SLAB)
        C[rows, :] = mm(order, EC[w].reshape(SLAB, D)).astype(BF)
    for i in range(4):
        rows = pl.ds(i * WIN, WIN)
        mixed = mm(A[rows, :], wout[...])
        centred = mixed - jnp.mean(mixed, axis=-1, keepdims=True)
        rstd = lax.rsqrt(jnp.mean(centred * centred, axis=-1, keepdims=True) + 1e-5)
        normed = centred * rstd
        up = C[rows, :].astype(F32)
        d_mixed = rstd * (
            up - jnp.mean(up, axis=-1, keepdims=True) - normed * jnp.mean(up * normed, axis=-1, keepdims=True)
        )
        d_mixed = d_mixed.astype(BF)
        DM[rows, :] = d_mixed
        DA[rows, :] = mm(d_mixed, wout[...], NT).astype(BF)

    sent = []

    def span(lo, hi):
        return pl.ds(lo * 128, (hi - lo) * 128)

    def to_core(part):
        return [
            remote(
                G.at[1 - core, :, :, :, :, span(lo, hi)],
                R0.at[:, :, :, :, span(lo, hi)],
                s0.at[part, n],
                r0.at[part, n],
                moved(at, core=1),
            )
            for n, (lo, hi) in enumerate(PARTS[part])
        ]

    def to_cube(part, flying):
        out = []
        for n, (lo, hi) in enumerate(PARTS[part]):
            flying[n].wait_recv()
            sent.append(flying[n])
            cols = span(lo, hi)
            CB[:, :, :, :, cols] = (G[core, :, :, :, :, cols] + R0[:, :, :, :, cols]).astype(BF)
            for k, (a, b, c) in enumerate(CUBE):
                steps = {
                    axis: far * (1 - 2 * n) * (1 - 2 * bit[axis]) for axis, far in (("x", a), ("y", b), ("z", c)) if far
                }
                place = [1 - bit[axis] if far else bit[axis] for axis, far in (("x", a), ("y", b), ("z", c))]
                out.append(
                    remote(
                        CB.at[place[0], place[1], place[2], :, cols],
                        RC.at[k, :, cols],
                        sc.at[part, n, k],
                        rc.at[part, n, k],
                        moved(at, **steps),
                    )
                )
        return out

    def take_cube(part, flying):
        for copy in reversed(flying):
            copy.wait_recv()
        sent.extend(flying)
        for c in range(PARTS[part][0][0], PARTS[part][1][1]):
            cols = span(c, c + 1)
            value = G[core, bit["x"], bit["y"], bit["z"], :, cols] + R0[bit["x"], bit["y"], bit["z"], :, cols]
            for k in range(len(CUBE)):
                value = value + RC[k, :, cols].astype(F32)
            F[c // 8, pl.ds(c % 8, 32, stride=8), :] = value

    def row(a, b, c):
        place = ((at["x"] // 2 + a) % 2) * 16 + ((at["y"] // 2 + b) % 4) * 4 + (at["z"] // 2 + c) % 4
        return pl.ds(pl.multiple_of(place * 8, 8), 8)

    def to_far(half):
        return [
            remote(
                F.at[half, row(a, b, c)],
                Q.at[half, n],
                sf.at[half, n],
                rf.at[half, n],
                moved(at, x=2 * a, y=2 * b, z=2 * c),
            )
            for n, (a, b, c) in enumerate(FAR)
        ]

    def take_far(half, flying):
        value = F[half, row(0, 0, 0), :]
        for n, copy in reversed(list(enumerate(flying))):
            copy.wait_recv()
            value = value + Q[half, n]
        return value * norm

    def backward(g, i):
        rows = pl.ds(i * WIN, WIN)
        q, k, v = parts(rows, g)
        d_att = stack_heads(DA[rows, g * 256 : (g + 1) * 256])
        d_probs = mm(v, d_att, NT)
        probs_b, d_scores = [], []
        for c in range(LANES // 128):
            cols = slice(c * 128, (c + 1) * 128)
            p = PT[i * 2 + g, :, cols]
            dp = d_probs[:, cols]
            probs_b.append(p.astype(BF))
            d_scores.append((p * (dp - jnp.sum(dp * p, axis=0, keepdims=True)) * SCALE).astype(BF))
        d_scores = jnp.concatenate(d_scores, axis=1)
        for c, part in enumerate((pick_heads(mm(d_scores, k, TN)), mm(d_scores, stack_heads(q)))):
            DP[rows, c * D + g * 256 : c * D + (g + 1) * 256] = part.astype(BF)
        if g == 0:
            d_values = [mm(jnp.concatenate(probs_b, axis=1), d_att)]
            d_values.append(mm(PT[i * 2 + 1].astype(BF), stack_heads(DA[rows, 256:D])))
            DP[rows, 2 * D : 3 * D] = jnp.concatenate(d_values, axis=1).astype(BF)

    def weight_grad(block, lo, hi):
        G[:, :, :, :, :, span(block, block + (hi - lo) // 128)] = mm(XO[...], DP[:, lo:hi]).reshape(
            2, 2, 2, 2, 32, hi - lo
        )

    G[:, :, :, :, :, 0:D] = mm(mm(owner, A[...], NT).astype(BF), DM[...]).reshape(2, 2, 2, 2, 32, D)
    core_out = to_core(0)
    relay_wait(2)
    relay_send(3)
    for i in range(4):
        backward(0, i)
    cube_out = to_cube(0, core_out)
    weight_grad(4, 0, 256)
    weight_grad(6, D, D + 256)
    weight_grad(8, 2 * D, 3 * D)
    core_first = to_core(1)
    relay_wait(3)
    for i in range(4):
        backward(1, i)
    weight_grad(12, 256, D)
    weight_grad(14, D + 256, 2 * D)
    core_second = to_core(2)

    back = one_hot(level_order, (SLAB, SLAB), swap=True)
    for w in range(2):
        grads = mm(DP[pl.ds(w * SLAB, SLAB), :], wqkv[...], NT).astype(BF)
        path[w] = mm(back, grads).astype(BF).reshape(path.shape[1:])
        if w == 0:
            cube_first = to_cube(1, core_first)
    cube_second = to_cube(2, core_second)
    take_cube(0, cube_out)
    backs = [
        remote(path.at[0, :, 3:6], own_path.at[6:18, 0:3], bs.at[0], br.at[0], near(0, 1)),
        remote(path.at[1, 0:6, 0:3], own_path.at[18:24, 3:6], bs.at[1], br.at[1], near(0, -1)),
        remote(path.at[1, 6:12, 0:3], own_path.at[0:6, 3:6], bs.at[2], br.at[2], near(1, -1)),
        remote(path.at[1, 6:12, 3:6], own_path.at[0:6, 0:3], bs.at[3], br.at[3], near(1, 0)),
        local(path.at[0, :, 0:3], own_path.at[6:18, 3:6], bl.at[0]),
        local(path.at[1, 0:6, 3:6], own_path.at[18:24, 0:3], bl.at[1]),
    ]
    take_cube(1, cube_first)
    far_first = to_far(0)
    take_cube(2, cube_second)
    far_second = to_far(1)
    for copy in backs:
        copy.wait()
    own[2].wait()

    def add(i, _):
        CT[i] = (CT[i].astype(F32) + own_path[i].astype(F32)).astype(BF)
        return 0

    lax.fori_loop(0, CT.shape[0], add, 0)
    out = local(CT, grad_tok, ws.at[3])
    low = take_far(0, far_first)
    for copy in sent + far_first + far_second:
        copy.wait_send()
    high = take_far(1, far_second)
    grad_out[...] = low[0:4]
    for n, block in enumerate(QKV_BLOCKS):
        grad_qkv[n : n + 1, :] = (low, high)[block // 8][block % 8 : block % 8 + 1]
    out.wait()


def block(tok, cot, wqkv, wout, norm):
    vm = pl.BlockSpec(memory_space=pltpu.VMEM)
    any_ = pl.BlockSpec(memory_space=pl.ANY)
    rows = pltpu.VMEM((TOK, D), BF)
    wide = pltpu.VMEM((TOK, 3 * D), BF)
    ext = pltpu.VMEM((2, 12, 6, 4, D), BF)
    dma = pltpu.SemaphoreType.DMA
    return pl.pallas_call(
        functools.partial(block_kernel, norm),
        out_shape=(
            jax.ShapeDtypeStruct(tok.shape, BF),
            jax.ShapeDtypeStruct((12, 128), F32),
            jax.ShapeDtypeStruct((4, 128), F32),
        ),
        in_specs=[any_] * 4,
        out_specs=(any_, vm, vm),
        scratch_shapes=[
            pltpu.VMEM(wqkv.shape, BF),
            pltpu.VMEM(wout.shape, BF),
            pltpu.VMEM(tok.shape, BF),
            pltpu.VMEM(tok.shape, BF),
            ext,
            ext,
            rows,
            pltpu.VMEM((D, TOK), BF),
            rows,
            wide,
            rows,
            rows,
            rows,
            wide,
            pltpu.VMEM((8, WIN, LANES), F32),
            ext,
            pltpu.VMEM((2, 2, 2, 2, 32, 4 * D), F32),
            pltpu.VMEM((2, 2, 2, 32, 4 * D), F32),
            pltpu.VMEM((2, 2, 2, 32, 4 * D), BF),
            pltpu.VMEM((len(CUBE), 32, 4 * D), BF),
            pltpu.VMEM((2, 32 * 8, 128), F32),
            pltpu.VMEM((2, len(FAR), 8, 128), F32),
            dma((4,)),
            dma((2, 4)),
            dma((2, 4)),
            dma((2, 2)),
            dma((4,)),
            dma((4,)),
            dma((2,)),
            dma((3, 2)),
            dma((3, 2)),
            dma((3, 2, len(CUBE))),
            dma((3, 2, len(CUBE))),
            dma((2, len(FAR))),
            dma((2, len(FAR))),
            pltpu.SemaphoreType.REGULAR((len(RELAY),)),
        ],
        compiler_params=pltpu.CompilerParams(collective_id=0, has_side_effects=True, vmem_limit_bytes=56 * 2**20),
        name="block",
    )(tok, cot, wqkv, wout)


def body(tokens, cotangent, w_qkv, w_out):
    count = tokens.shape[0] * tokens.shape[1] * tokens.shape[2] * lax.axis_size("lon") * lax.axis_size("lat")
    grad_tokens, grad_qkv, grad_out = block(tokens, cotangent, w_qkv, w_out, 1.0 / math.sqrt(count))
    return grad_tokens, grad_qkv.reshape(-1), grad_out.reshape(-1)


def solution(mesh):
    in_specs = (P("lon", "lat", None, None), P("lon", "lat", None, None), P(), P())
    out_specs = (P("lon", "lat", None, None), P(("lon", "lat")), P(("lon", "lat")))
    return jax.shard_map(body, mesh=mesh, in_specs=in_specs, out_specs=out_specs, check_vma=False)
```

```python
import functools
import math

import jax
import jax.numpy as jnp
from jax import lax
from jax.experimental import pallas as pl
from jax.experimental.pallas import tpu as pltpu
from jax.sharding import PartitionSpec as P

D = 512
H = 16
E = 32
WIN = 144
SLAB = 2 * WIN
TOK = 2 * SLAB
GROUP = 8
LANES = GROUP * WIN
SCALE = 1.0 / math.sqrt(E)
BF = jnp.bfloat16
F32 = jnp.float32
MESH = pl.DeviceIdType.MESH
NN = (((1,), (0,)), ((), ()))
NT = (((1,), (1,)), ((), ()))
TN = (((0,), (0,)), ((), ()))


def mm(a, b, dims=NN):
    return lax.dot_general(a, b, dims, preferred_element_type=F32)


def near(lon, lat):
    n_lon, n_lat = lax.axis_size("lon"), lax.axis_size("lat")
    return ((lax.axis_index("lon") + lon + n_lon) % n_lon, (lax.axis_index("lat") + lat + n_lat) % n_lat)


HALO = ((0, 1), (0, -1), (1, 0), (-1, 0), (1, -1), (-1, 1))
SIZES = {"x": 4, "y": 8, "z": 8}
CUBE = tuple((a, b, c) for a in (1, 0) for b in (1, 0) for c in (1, 0) if a + b + c)
FAR = tuple((a, b, c) for a in (1, 0) for b in (2, 1, 3, 0) for c in (2, 1, 3, 0) if a + b + c)
RELAY = (("y", (2, -2)), ("z", (2, -2)), ("z", (2, -2)), ("x", (2,)))
PARTS = (((0, 2), (2, 4)), ((4, 8), (8, 12)), ((12, 14), (14, 16)))
QKV_BLOCKS = (4, 5, 12, 13, 6, 7, 14, 15, 8, 9, 10, 11)


def position():
    lon, lat = lax.axis_index("lon"), lax.axis_index("lat")
    return {"x": lon // 16, "y": lon % 8, "z": (lat // 2) * 2 + (lon // 8) % 2, "core": lat % 2}


def device(at):
    return (at["x"] * 16 + (at["z"] % 2) * 8 + at["y"], (at["z"] // 2) * 2 + at["core"])


def moved(at, **steps):
    new = dict(at)
    for axis, step in steps.items():
        size = SIZES.get(axis, 2)
        new[axis] = (at[axis] + step + size) % size
    return device(new)


def lane_head():
    return lax.broadcasted_iota(jnp.int32, (WIN, 256), 1) // E


def stack_heads(x):
    lane = lane_head()
    zero = jnp.zeros_like(x)
    return jnp.concatenate([jnp.where(lane == h, x, zero) for h in range(GROUP)], axis=0)


def pick_heads(r):
    lane = lane_head()
    out = r[0:WIN]
    for h in range(1, GROUP):
        out = jnp.where(lane == h, r[h * WIN : (h + 1) * WIN], out)
    return out


def level_order(rows, natural):
    return natural == 4 * (rows % 72) + (rows // 72 + 1) % 4


def owner_order(i, p):
    x = 2 * ((p // 16) % 2) + (p // 128) % 2
    y = 2 * ((p // 4) % 4) + (p // 64) % 2
    return i == x * 128 + ((p // 32) % 2) * 64 + y * 8 + (p % 4) * 2 + p // 256


def one_hot(relation, shape, swap=False):
    a = lax.broadcasted_iota(jnp.int32, shape, 1 if swap else 0)
    b = lax.broadcasted_iota(jnp.int32, shape, 0 if swap else 1)
    return jnp.where(relation(a, b), 1.0, 0.0).astype(BF)


def region(pos, split_level, split_lat):
    return (pos // 72) * split_level + 2 * split_lat * ((pos % 6) // 3)


def signal(sem, to):
    pl.semaphore_signal(sem, inc=1, device_id=to, device_id_type=MESH)


def remote(src, dst, send, recv, to):
    copy = pltpu.make_async_remote_copy(
        src_ref=src, dst_ref=dst, send_sem=send, recv_sem=recv, device_id=to, device_id_type=MESH
    )
    copy.start()
    return copy


def local(src, dst, sem):
    copy = pltpu.make_async_copy(src, dst, sem)
    copy.start()
    return copy


def block_kernel(norm, tok, cot, wqkv_in, wout_in, grad_tok, grad_qkv, grad_out, *scratch):
    (wqkv, wout, CT, own_path, ET, EC, X, XO, C, PR, A, DM, DA, DP, PT, path, G, R0, CB, RC, F, Q) = scratch[:22]
    (ws, hs, hr, hl, bs, br, bl, s0, r0, sc, rc, sf, rf, relay) = scratch[22:]
    at = position()
    bit = {axis: at[axis] % 2 for axis in SIZES}
    core = at["core"]
    lat = lax.axis_index("lat")
    last = lax.axis_size("lat") - 1

    greeted = [near(*step) for step in HALO] + [moved(at, core=1)]
    for a, b, c in CUBE:
        for sense in (1, -1):
            steps = {axis: sense * far * (1 - 2 * bit[axis]) for axis, far in (("x", a), ("y", b), ("z", c))}
            greeted.append(moved(at, **steps))
    greeted += [moved(at, **{axis: step}) for axis, steps in RELAY[1:] + RELAY[:1] for step in steps][2:]
    barrier = pltpu.get_barrier_semaphore()
    for other in greeted:
        signal(barrier, other)
    own = [local(wqkv_in, wqkv, ws.at[0]), local(wout_in, wout, ws.at[1]), local(cot, CT, ws.at[2])]
    pl.semaphore_wait(barrier, len(greeted))

    come = []
    for a, (src, ext) in enumerate(((tok, ET), (cot, EC))):
        come.append(
            (
                local(src.at[6:18, 3:6], ext.at[0, :, 0:3], hl.at[a, 0]),
                remote(src.at[6:18, 0:3], ext.at[0, :, 3:6], hs.at[a, 0], hr.at[a, 0], near(0, -1)),
            )
        )
        come.append(
            (
                local(src.at[18:24, 0:3], ext.at[1, 0:6, 3:6], hl.at[a, 1]),
                remote(src.at[18:24, 3:6], ext.at[1, 0:6, 0:3], hs.at[a, 1], hr.at[a, 1], near(0, 1)),
                remote(src.at[0:6, 3:6], ext.at[1, 6:12, 0:3], hs.at[a, 2], hr.at[a, 2], near(-1, 1)),
                remote(src.at[0:6, 0:3], ext.at[1, 6:12, 3:6], hs.at[a, 3], hr.at[a, 3], near(-1, 0)),
            )
        )

    def relay_send(n):
        axis, steps = RELAY[n]
        for step in steps:
            signal(relay.at[n], moved(at, **{axis: step}))

    def relay_wait(n):
        pl.semaphore_wait(relay.at[n], len(RELAY[n][1]))

    relay_send(0)
    own[0].wait()
    order = one_hot(level_order, (SLAB, SLAB))
    owner = one_hot(owner_order, (D, D), swap=True)

    def parts(rows, g):
        return [PR[rows, c * D + g * 256 : c * D + (g + 1) * 256] for c in range(3)]

    def forward(i):
        rows = pl.ds(i * WIN, WIN)
        split_lat = jnp.where(lat == (last if i < 2 else 0), 1, 0)
        key_region = region(lax.broadcasted_iota(jnp.int32, (WIN, 128), 0), i % 2, split_lat)
        for g in range(2):
            q, k, v = parts(rows, g)
            scores = mm(k, stack_heads(q), NT)
            probs_b = []
            for c in range(LANES // 128):
                cols = slice(c * 128, (c + 1) * 128)
                pos = lax.broadcasted_iota(jnp.int32, (1, 128), 1) + c * 128
                allowed = key_region == region(pos % WIN, i % 2, split_lat)
                s = jnp.where(allowed, scores[:, cols] * SCALE, -1e30)
                e = jnp.exp(s - jnp.max(s, axis=0, keepdims=True))
                p = e * (1.0 / jnp.sum(e, axis=0, keepdims=True))
                PT[i * 2 + g, :, cols] = p
                probs_b.append(p.astype(BF))
            probs_b = jnp.concatenate(probs_b, axis=1)
            A[rows, g * 256 : (g + 1) * 256] = pick_heads(mm(probs_b, v, TN)).astype(BF)

    for w in range(2):
        for copy in come[w]:
            copy.wait()
        rows = pl.ds(w * SLAB, SLAB)
        X[rows, :] = mm(order, ET[w].reshape(SLAB, D)).astype(BF)
        for c in range(3):
            cols = pl.ds(c * D, D)
            PR[rows, cols] = mm(X[rows, :], wqkv[:, cols]).astype(BF)
        for i in range(2 * w, 2 * w + 2):
            forward(i)
        relay_wait(w)
        relay_send(w + 1)

    XO[...] = mm(owner, X[...], NT).astype(BF)
    own[1].wait()
    for w in range(2):
        for copy in come[2 + w]:
            copy.wait()
        rows = pl.ds(w * SLAB, SLAB)
        C[rows, :] = mm(order, EC[w].reshape(SLAB, D)).astype(BF)
    for i in range(4):
        rows = pl.ds(i * WIN, WIN)
        mixed = mm(A[rows, :], wout[...])
        centred = mixed - jnp.mean(mixed, axis=-1, keepdims=True)
        rstd = lax.rsqrt(jnp.mean(centred * centred, axis=-1, keepdims=True) + 1e-5)
        normed = centred * rstd
        up = C[rows, :].astype(F32)
        d_mixed = rstd * (
            up - jnp.mean(up, axis=-1, keepdims=True) - normed * jnp.mean(up * normed, axis=-1, keepdims=True)
        )
        d_mixed = d_mixed.astype(BF)
        DM[rows, :] = d_mixed
        DA[rows, :] = mm(d_mixed, wout[...], NT).astype(BF)

    sent = []

    def span(lo, hi):
        return pl.ds(lo * 128, (hi - lo) * 128)

    def to_core(part):
        return [
            remote(
                G.at[1 - core, :, :, :, :, span(lo, hi)],
                R0.at[:, :, :, :, span(lo, hi)],
                s0.at[part, n],
                r0.at[part, n],
                moved(at, core=1),
            )
            for n, (lo, hi) in enumerate(PARTS[part])
        ]

    def to_cube(part, flying):
        out = []
        for n, (lo, hi) in enumerate(PARTS[part]):
            flying[n].wait_recv()
            sent.append(flying[n])
            cols = span(lo, hi)
            CB[:, :, :, :, cols] = (G[core, :, :, :, :, cols] + R0[:, :, :, :, cols]).astype(BF)
            for k, (a, b, c) in enumerate(CUBE):
                steps = {
                    axis: far * (1 - 2 * n) * (1 - 2 * bit[axis]) for axis, far in (("x", a), ("y", b), ("z", c)) if far
                }
                place = [1 - bit[axis] if far else bit[axis] for axis, far in (("x", a), ("y", b), ("z", c))]
                out.append(
                    remote(
                        CB.at[place[0], place[1], place[2], :, cols],
                        RC.at[k, :, cols],
                        sc.at[part, n, k],
                        rc.at[part, n, k],
                        moved(at, **steps),
                    )
                )
        return out

    def take_cube(part, flying):
        for copy in reversed(flying):
            copy.wait_recv()
        sent.extend(flying)
        for c in range(PARTS[part][0][0], PARTS[part][1][1]):
            cols = span(c, c + 1)
            value = G[core, bit["x"], bit["y"], bit["z"], :, cols] + R0[bit["x"], bit["y"], bit["z"], :, cols]
            for k in range(len(CUBE)):
                value = value + RC[k, :, cols].astype(F32)
            F[c // 8, pl.ds(c % 8, 32, stride=8), :] = value

    def row(a, b, c):
        place = ((at["x"] // 2 + a) % 2) * 16 + ((at["y"] // 2 + b) % 4) * 4 + (at["z"] // 2 + c) % 4
        return pl.ds(pl.multiple_of(place * 8, 8), 8)

    def to_far(half):
        return [
            remote(
                F.at[half, row(a, b, c)],
                Q.at[half, n],
                sf.at[half, n],
                rf.at[half, n],
                moved(at, x=2 * a, y=2 * b, z=2 * c),
            )
            for n, (a, b, c) in enumerate(FAR)
        ]

    def take_far(half, flying):
        value = F[half, row(0, 0, 0), :]
        for n, copy in reversed(list(enumerate(flying))):
            copy.wait_recv()
            value = value + Q[half, n]
        return value * norm

    def backward(g, i):
        rows = pl.ds(i * WIN, WIN)
        q, k, v = parts(rows, g)
        d_att = stack_heads(DA[rows, g * 256 : (g + 1) * 256])
        d_probs = mm(v, d_att, NT)
        probs_b, d_scores = [], []
        for c in range(LANES // 128):
            cols = slice(c * 128, (c + 1) * 128)
            p = PT[i * 2 + g, :, cols]
            dp = d_probs[:, cols]
            probs_b.append(p.astype(BF))
            d_scores.append((p * (dp - jnp.sum(dp * p, axis=0, keepdims=True)) * SCALE).astype(BF))
        d_scores = jnp.concatenate(d_scores, axis=1)
        for c, part in enumerate((pick_heads(mm(d_scores, k, TN)), mm(d_scores, stack_heads(q)))):
            DP[rows, c * D + g * 256 : c * D + (g + 1) * 256] = part.astype(BF)
        if g == 0:
            d_values = [mm(jnp.concatenate(probs_b, axis=1), d_att)]
            d_values.append(mm(PT[i * 2 + 1].astype(BF), stack_heads(DA[rows, 256:D])))
            DP[rows, 2 * D : 3 * D] = jnp.concatenate(d_values, axis=1).astype(BF)

    def weight_grad(block, lo, hi):
        G[:, :, :, :, :, span(block, block + (hi - lo) // 128)] = mm(XO[...], DP[:, lo:hi]).reshape(
            2, 2, 2, 2, 32, hi - lo
        )

    G[:, :, :, :, :, 0:D] = mm(mm(owner, A[...], NT).astype(BF), DM[...]).reshape(2, 2, 2, 2, 32, D)
    core_out = to_core(0)
    relay_wait(2)
    relay_send(3)
    for i in range(4):
        backward(0, i)
    cube_out = to_cube(0, core_out)
    weight_grad(4, 0, 256)
    weight_grad(6, D, D + 256)
    weight_grad(8, 2 * D, 3 * D)
    core_first = to_core(1)
    relay_wait(3)
    for i in range(4):
        backward(1, i)
    weight_grad(12, 256, D)
    weight_grad(14, D + 256, 2 * D)
    core_second = to_core(2)

    back = one_hot(level_order, (SLAB, SLAB), swap=True)
    backs = []
    for w in range(2):
        grads = mm(DP[pl.ds(w * SLAB, SLAB), :], wqkv[...], NT).astype(BF)
        path[w] = mm(back, grads).astype(BF).reshape(path.shape[1:])
        if w == 0:
            backs += [
                remote(path.at[0, :, 3:6], own_path.at[6:18, 0:3], bs.at[0], br.at[0], near(0, 1)),
                local(path.at[0, :, 0:3], own_path.at[6:18, 3:6], bl.at[0]),
            ]
        else:
            backs += [
                remote(path.at[1, 0:6, 0:3], own_path.at[18:24, 3:6], bs.at[1], br.at[1], near(0, -1)),
                remote(path.at[1, 6:12, 0:3], own_path.at[0:6, 3:6], bs.at[2], br.at[2], near(1, -1)),
                remote(path.at[1, 6:12, 3:6], own_path.at[0:6, 0:3], bs.at[3], br.at[3], near(1, 0)),
                local(path.at[1, 0:6, 3:6], own_path.at[18:24, 0:3], bl.at[1]),
            ]
    cube_first = to_cube(1, core_first)
    cube_second = to_cube(2, core_second)
    take_cube(0, cube_out)
    take_cube(1, cube_first)
    far_first = to_far(0)
    take_cube(2, cube_second)
    far_second = to_far(1)
    for copy in backs:
        copy.wait()
    own[2].wait()

    def add(i, _):
        CT[i] = (CT[i].astype(F32) + own_path[i].astype(F32)).astype(BF)
        return 0

    lax.fori_loop(0, CT.shape[0], add, 0)
    out = local(CT, grad_tok, ws.at[3])
    low = take_far(0, far_first)
    for copy in sent + far_first + far_second:
        copy.wait_send()
    high = take_far(1, far_second)
    grad_out[...] = low[0:4]
    for n, block in enumerate(QKV_BLOCKS):
        grad_qkv[n : n + 1, :] = (low, high)[block // 8][block % 8 : block % 8 + 1]
    out.wait()


def block(tok, cot, wqkv, wout, norm):
    vm = pl.BlockSpec(memory_space=pltpu.VMEM)
    any_ = pl.BlockSpec(memory_space=pl.ANY)
    rows = pltpu.VMEM((TOK, D), BF)
    wide = pltpu.VMEM((TOK, 3 * D), BF)
    ext = pltpu.VMEM((2, 12, 6, 4, D), BF)
    dma = pltpu.SemaphoreType.DMA
    return pl.pallas_call(
        functools.partial(block_kernel, norm),
        out_shape=(
            jax.ShapeDtypeStruct(tok.shape, BF),
            jax.ShapeDtypeStruct((12, 128), F32),
            jax.ShapeDtypeStruct((4, 128), F32),
        ),
        in_specs=[any_] * 4,
        out_specs=(any_, vm, vm),
        scratch_shapes=[
            pltpu.VMEM(wqkv.shape, BF),
            pltpu.VMEM(wout.shape, BF),
            pltpu.VMEM(tok.shape, BF),
            pltpu.VMEM(tok.shape, BF),
            ext,
            ext,
            rows,
            pltpu.VMEM((D, TOK), BF),
            rows,
            wide,
            rows,
            rows,
            rows,
            wide,
            pltpu.VMEM((8, WIN, LANES), F32),
            ext,
            pltpu.VMEM((2, 2, 2, 2, 32, 4 * D), F32),
            pltpu.VMEM((2, 2, 2, 32, 4 * D), F32),
            pltpu.VMEM((2, 2, 2, 32, 4 * D), BF),
            pltpu.VMEM((len(CUBE), 32, 4 * D), BF),
            pltpu.VMEM((2, 32 * 8, 128), F32),
            pltpu.VMEM((2, len(FAR), 8, 128), F32),
            dma((4,)),
            dma((2, 4)),
            dma((2, 4)),
            dma((2, 2)),
            dma((4,)),
            dma((4,)),
            dma((2,)),
            dma((3, 2)),
            dma((3, 2)),
            dma((3, 2, len(CUBE))),
            dma((3, 2, len(CUBE))),
            dma((2, len(FAR))),
            dma((2, len(FAR))),
            pltpu.SemaphoreType.REGULAR((len(RELAY),)),
        ],
        compiler_params=pltpu.CompilerParams(collective_id=0, has_side_effects=True, vmem_limit_bytes=56 * 2**20),
        name="block",
    )(tok, cot, wqkv, wout)


def body(tokens, cotangent, w_qkv, w_out):
    count = tokens.shape[0] * tokens.shape[1] * tokens.shape[2] * lax.axis_size("lon") * lax.axis_size("lat")
    grad_tokens, grad_qkv, grad_out = block(tokens, cotangent, w_qkv, w_out, 1.0 / math.sqrt(count))
    return grad_tokens, grad_qkv.reshape(-1), grad_out.reshape(-1)


def solution(mesh):
    in_specs = (P("lon", "lat", None, None), P("lon", "lat", None, None), P(), P())
    out_specs = (P("lon", "lat", None, None), P(("lon", "lat")), P(("lon", "lat")))
    return jax.shard_map(body, mesh=mesh, in_specs=in_specs, out_specs=out_specs, check_vma=False)
```
